128 devices in a mesh: prow: 8 (over y, core), pcol: 16 (over z, x).
Axes of the slice: x: 4, y: 4, z: 4, core: 2. Of those that a mesh axis runs over, the one named last changes fastest.
Arguments:
- spectra: bfloat16 [80, 128, 16, 2, 128], P('pcol', 'prow'), may hold values from -6 to 6
- tile_list: int32 [8, 16, 10, 2], P('prow', 'pcol'), may hold values from 0 to 79, as said below
- tile_count: int32 [8, 16], P('prow', 'pcol'), may hold values from 0 to 10, as said below
- observed: bfloat16 [8, 16, 10, 16, 2, 128, 128], P('prow', 'pcol'), may hold values from -0.59765625 to 0.59765625
Outputs:
- gradient: float32 [80, 128, 16, 2, 128], P('pcol', 'prow')
The draws below stay inside these ranges and needn't reach their ends.
Inputs may be any that keep to these rules, and one draw needn't show every extreme that they name: Entries are channel block numbers; the row block of every entry of tile_list[r, q] lies among the 5 blocks of pcol index q; every pair (a, b) with a <= b <= a + 8 and b < 80 appears exactly once among the live entries of the 8 lists of that pcol index; entries past tile_count are (q * 5, q * 5). `tile_count`: loads differ strongly between the devices of one block column; in every draw some device has a full list of 10 live tiles.
All inputs are finite; a program needn't handle non-finite values.
Results may differ from the reference program's by a relative error of at most 0.0075.
Values may be sent and summed in bfloat16 or wider, within the bound.
No kernel may reach another device: no remote copies, remote signals or barrier semaphores. Data moves between devices by JAX's collectives and lax.ppermute only.
A program may use at most 192 MiB of HBM per device.

```python
import jax
import jax.numpy as jnp
from jax import lax

CB = 128
BAND = 8
FREQ = 16
WIN = 128
BPC = 5
NB = 80
SLOTS = 10
N_PROW = 8
N_PCOL = 16


def assign_tiles(key):
    candidates = BPC * (BAND + 1)
    block_count = BPC * N_PCOL
    levels = jnp.arange(N_PROW + 1, dtype=jnp.int32)
    stops = candidates * levels * (levels + 1) // (N_PROW * (N_PROW + 1))
    slot_ids = jnp.arange(SLOTS, dtype=jnp.int32)

    def column_lists(column):
        column_key = jax.random.fold_in(key, column)
        ranks = jax.random.permutation(jax.random.fold_in(column_key, 1), N_PROW)
        ordering = jax.random.permutation(jax.random.fold_in(column_key, 2), candidates)
        starts = stops[ranks]
        counts = stops[ranks + 1] - starts
        places = jnp.minimum(starts[:, None] + slot_ids[None, :], candidates - 1)
        chosen = ordering[places]
        first_ids = column * BPC + chosen // (BAND + 1)
        second_ids = first_ids + chosen % (BAND + 1)
        live = (slot_ids[None, :] < counts[:, None]) & (second_ids < block_count)
        arrange = jnp.argsort(1 - live.astype(jnp.int32), axis=1, stable=True)
        first_ids = jnp.take_along_axis(first_ids, arrange, axis=1)
        second_ids = jnp.take_along_axis(second_ids, arrange, axis=1)
        live = jnp.take_along_axis(live, arrange, axis=1)
        padding = column * BPC
        first_ids = jnp.where(live, first_ids, padding)
        second_ids = jnp.where(live, second_ids, padding)
        return (jnp.stack([first_ids, second_ids], axis=-1).astype(jnp.int32), jnp.sum(live.astype(jnp.int32), axis=1))
    lists, counts = jax.vmap(column_lists)(jnp.arange(N_PCOL, dtype=jnp.int32))
    return (jnp.transpose(lists, (1, 0, 2, 3)), jnp.transpose(counts, (1, 0)))


def draw_tile_list(key, part):
    lists, counts = assign_tiles(key)
    return lists


def draw_tile_count(key, part):
    lists, counts = assign_tiles(key)
    return counts


def shard_levels(stream_key, extent, cuts, low, largest):
    loudness, own = 1.0, jax.random.fold_in(stream_key, 6)
    for dim, shards_of in cuts:
        heights = jnp.exp(jax.random.uniform(jax.random.fold_in(own, dim), (shards_of,), jnp.float32, low / len(cuts), largest / len(cuts)))
        loudness = loudness * jnp.repeat(heights, extent[dim] // shards_of).reshape([-1 if axis == dim else 1 for axis in range(len(extent))])
    return loudness


def bell_draw(stream_key, extent, scale, limit, split=(), kind=jnp.bfloat16):
    level = shard_levels(stream_key, extent, split, -0.22, 0.18) if split else 1.0
    entries = jax.random.normal(stream_key, extent, jnp.float32) * scale * level
    return jnp.minimum(jnp.maximum(entries, -limit), limit).astype(kind)


def setup_inputs(seed: int = 0) -> dict:
    seeds = jax.random.split(jax.random.key(seed), 5)
    return {
        "spectra": bell_draw(seeds[0], (NB, CB, FREQ, 2, WIN), 1.0, 6.0, ((0, 16), (1, 8))),
        "tile_list": draw_tile_list(jax.random.fold_in(seeds[4], 71), 0),
        "tile_count": draw_tile_count(jax.random.fold_in(seeds[4], 71), 0),
        "observed": bell_draw(seeds[3], (N_PROW, N_PCOL, SLOTS, FREQ, 2, CB, CB), 0.1, 0.59765625, ((0, 8), (1, 16))),
    }


eps_power = 1e-06
misfit_scale = 0.1

def whiten(spectra):
    values = spectra.astype(jnp.float32)
    power = lax.optimization_barrier(jnp.sum(values * values, axis=(3, 4), keepdims=True)) / values.shape[4]
    factor = lax.rsqrt(power + eps_power)
    return (values, factor)

def tile_terms(row_block, col_block, observed_tile, tile_mask):
    row_data = row_block.astype(jnp.float32)
    col_data = col_block.astype(jnp.float32)
    windows = row_data.shape[3]
    col_turn = jnp.stack([col_data[:, :, 1], -col_data[:, :, 0]], axis=2)
    row_turn = jnp.stack([-row_data[:, :, 1], row_data[:, :, 0]], axis=2)
    real_part = jnp.einsum('ifkw,jfkw->fij', row_data, col_data) / windows
    imag_part = jnp.einsum('ifkw,jfkw->fij', row_data, col_turn) / windows
    resid = jnp.stack([real_part, imag_part], axis=1) - observed_tile.astype(jnp.float32)
    scaled = resid / misfit_scale
    slope = resid / jnp.sqrt(1.0 + scaled * scaled) * tile_mask
    slope = slope.astype(jnp.bfloat16).astype(jnp.float32)
    slope_real = slope[:, 0]
    slope_imag = slope[:, 1]
    row_grad = jnp.einsum('fij,jfkw->ifkw', slope_real, col_data) + jnp.einsum('fij,jfkw->ifkw', slope_imag, col_turn)
    col_grad = jnp.einsum('fij,ifkw->jfkw', slope_real, row_data) + jnp.einsum('fij,ifkw->jfkw', slope_imag, row_turn)
    return (row_grad, col_grad)

def reference(spectra, tile_list, tile_count, observed):
    values, factor = whiten(spectra)
    whitened = (values * factor).astype(jnp.bfloat16)
    block_count = spectra.shape[0]
    width = spectra.shape[1]
    reach = BAND + 1
    flat_obs = observed.reshape((-1,) + observed.shape[3:])
    slot_count = tile_list.shape[2]
    live = jnp.arange(slot_count, dtype=jnp.int32)[None, None, :] < tile_count[:, :, None]
    first_ids = tile_list[..., 0]
    second_ids = tile_list[..., 1]
    row_place = jnp.where(live, first_ids, block_count).astype(jnp.int32)
    off_place = jnp.where(live, second_ids - first_ids, 0).astype(jnp.int32)
    flat_ids = jnp.arange(first_ids.size, dtype=jnp.int32).reshape(first_ids.shape)
    table = jnp.zeros((block_count, reach), jnp.int32).at[row_place.reshape(-1), off_place.reshape(-1)].set(flat_ids.reshape(-1), mode='drop')
    upper_mask = (lax.broadcasted_iota(jnp.int32, (width, width), 1) > lax.broadcasted_iota(jnp.int32, (width, width), 0)).astype(jnp.float32)

    def per_block(total, block_id):
        row_block = whitened[block_id]
        for distance in range(reach):
            other_id = jnp.minimum(block_id + distance, block_count - 1).astype(jnp.int32)
            valid = (block_id + distance < block_count).astype(jnp.float32)
            if distance == 0:
                tile_mask = upper_mask * valid
            else:
                tile_mask = jnp.ones((width, width), jnp.float32) * valid
            row_grad, col_grad = tile_terms(row_block, whitened[other_id], flat_obs[table[block_id, distance]], tile_mask)
            total = total.at[block_id].add(row_grad)
            total = total.at[other_id].add(col_grad)
        return (total, None)
    start_total = jnp.zeros(spectra.shape, jnp.float32)
    total, _ = lax.scan(per_block, start_total, jnp.arange(block_count, dtype=jnp.int32))
    inner = lax.optimization_barrier(jnp.sum(total * values, axis=(3, 4), keepdims=True)) / spectra.shape[4]
    return factor * total - values * (factor * factor * factor) * inner
```

```python
import functools

import jax
import jax.numpy as jnp
from jax import lax
from jax.experimental import pallas as pl
from jax.experimental.pallas import tpu as pltpu
from jax.sharding import PartitionSpec as P

BAND = 8
EPS = 1e-06
CURVE = 100.0


def turn(block):
    half = block.shape[-1] // 2
    return jnp.concatenate([block[:, half:], -block[:, :half]], axis=1)


def tile_kernel(slots, meta, obs_own, *rest):
    others = rest[:7]
    own, near, far, grad_own, grad_near, grad_far = rest[7:13]
    order, held, stack, back, grad, first, second, sems = rest[13:]
    blocks = own.shape[0]
    reach = far.shape[0]
    width = own.shape[1]
    total = 2 * blocks + reach
    copies = []
    for k, piece in enumerate((obs_own,) + others):
        copies.append(pltpu.make_async_copy(piece, held.at[pl.ds(k * slots, slots)], sems.at[k]))
        copies[-1].start()

    live = 0
    for k in range(8):

        def put(s, at, k=k):
            order[0, at] = meta[k, 1 + 2 * s]
            order[1, at] = meta[k, 2 + 2 * s]
            order[2, at] = k * slots + s
            return at + 1

        live = lax.fori_loop(0, meta[k, 0], put, live)
    for extra in range(3):
        for row in range(3):
            order[row, live + extra] = 0

    for n in range(total):
        if n < blocks:
            block = own[n]
        elif n < 2 * blocks:
            block = near[n - blocks]
        else:
            block = far[n - 2 * blocks]
        turned = turn(block)
        stack[n, :width] = block
        stack[n, width:] = turned
        if n < blocks:
            back[n, :width] = block
            back[n, width:] = -turned
    grad[...] = jnp.zeros_like(grad)
    for copy in copies:
        copy.wait()

    gap = lax.broadcasted_iota(jnp.int32, (width, width), 1) - lax.broadcasted_iota(
        jnp.int32, (width, width), 0
    )

    def slope_of(t, into):
        a = order[0, t]
        b = order[1, t]
        spot = order[2, t]
        least = jnp.where(t < live, jnp.where(a == b, 0, -width), width)
        sums = lax.dot_general(
            stack[a, :width], stack[b], (((1,), (1,)), ((), ())), preferred_element_type=jnp.float32
        )
        keep = gap > least
        for part in range(2):
            seen = held[spot, part].astype(jnp.float32) * width
            diff = sums[:, part * width : (part + 1) * width] - seen
            slope = diff * lax.rsqrt(diff * diff * CURVE + float(width * width))
            into[part * width : (part + 1) * width] = jnp.where(keep, slope, 0.0).astype(jnp.bfloat16)

    def grads_of(t, slope):
        a = order[0, t]
        b = order[1, t]
        both = slope[...]
        wide = jnp.concatenate([both[:width], both[width:]], axis=1)
        row = jnp.dot(wide, stack[b], preferred_element_type=jnp.float32)
        col = lax.dot_general(
            both, back[a], (((0,), (0,)), ((), ())), preferred_element_type=jnp.float32
        )
        grad[a] += row
        grad[b] += col

    slope_of(0, first)

    def pair(m, carry):
        t = 2 * m
        slope_of(t + 1, second)
        grads_of(t, first)
        slope_of(t + 2, first)
        grads_of(t + 1, second)
        return carry

    lax.fori_loop(0, (live + 1) // 2, pair, 0)
    grad_own[...] = grad[:blocks]
    grad_near[...] = grad[blocks : 2 * blocks].astype(jnp.bfloat16)
    grad_far[...] = grad[2 * blocks :].astype(jnp.bfloat16)


def tile_call(meta, pieces, own, near, far):
    slots = pieces[0].shape[0]
    blocks, width, depth = own.shape
    reach = far.shape[0]
    total = 2 * blocks + reach
    vmem = pl.BlockSpec(memory_space=pltpu.VMEM)
    return pl.pallas_call(
        functools.partial(tile_kernel, slots),
        out_shape=(
            jax.ShapeDtypeStruct((blocks, width, depth), jnp.float32),
            jax.ShapeDtypeStruct((blocks, width, depth), jnp.bfloat16),
            jax.ShapeDtypeStruct((reach, width, depth), jnp.bfloat16),
        ),
        in_specs=[pl.BlockSpec(memory_space=pltpu.SMEM)]
        + [pl.BlockSpec(memory_space=pl.ANY)] * 8
        + [vmem] * 3,
        out_specs=(vmem, vmem, vmem),
        scratch_shapes=[
            pltpu.SMEM((3, 8 * slots + 8), jnp.int32),
            pltpu.VMEM((8 * slots, 2, width, width), jnp.bfloat16),
            pltpu.VMEM((total, 2 * width, depth), jnp.bfloat16),
            pltpu.VMEM((blocks, 2 * width, depth), jnp.bfloat16),
            pltpu.VMEM((total, width, depth), jnp.float32),
            pltpu.VMEM((2 * width, width), jnp.bfloat16),
            pltpu.VMEM((2 * width, width), jnp.bfloat16),
            pltpu.SemaphoreType.DMA((8,)),
        ],
        compiler_params=pltpu.CompilerParams(vmem_limit_bytes=40 * 1024 * 1024),
        cost_estimate=pl.CostEstimate(
            flops=45 * 6 * width * depth * depth, bytes_accessed=8 * 1024 * 1024, transcendentals=0
        ),
    )(meta, *pieces, own, near, far)


def final_kernel(spectra, own, near, far, out):
    blocks = own.shape[0]
    reach = far.shape[0]
    scale = 2.0 / spectra.shape[-1]
    for n in range(blocks):
        values = spectra[n].astype(jnp.float32)
        power = jnp.sum(values * values, axis=1, keepdims=True) * scale
        factor = lax.rsqrt(power + EPS)
        total = own[n] + near[n].astype(jnp.float32)
        if n < reach:
            total = total + far[n].astype(jnp.float32)
        inner = jnp.sum(total * values, axis=1, keepdims=True) * scale
        grad = factor * total - values * (factor * factor * factor * inner)
        out[n] = grad.astype(jnp.bfloat16)


def final_call(spectra, own, near, far):
    vmem = pl.BlockSpec(memory_space=pltpu.VMEM)
    return pl.pallas_call(
        final_kernel,
        out_shape=jax.ShapeDtypeStruct(spectra.shape, jnp.bfloat16),
        in_specs=[vmem] * 4,
        out_specs=vmem,
        compiler_params=pltpu.CompilerParams(vmem_limit_bytes=40 * 1024 * 1024),
    )(spectra, own, near, far)


HOPS = ((1, 0), (3, 0), (1, 1), (3, 1), (2, 0), (2, 1), (0, 1))


def across(values, step, flip):
    chips = lax.axis_size("prow") // 2
    route = [
        (2 * y + c, 2 * ((y + step) % chips) + (c ^ flip)) for y in range(chips) for c in range(2)
    ]
    return lax.ppermute(values, "prow", route)


def along(values, distance):
    devices = range(lax.axis_size("pcol"))
    route = [(i - distance, i) for i in devices if i - distance in devices]
    return lax.ppermute(values, "pcol", route)


def local(spectra, tile_list, tile_count, observed):
    blocks, share, bins, parts, windows = spectra.shape
    slots = tile_list.shape[2]
    width = 8 * share
    me = lax.axis_index("prow")
    chip = me // 2
    core = me % 2
    base = lax.axis_index("pcol") * blocks
    obs = observed[0, 0]

    targets = [(chip + step) % 4 * 2 + (core ^ flip) for step, flip in HOPS]
    sources = [(chip - step) % 4 * 2 + (core ^ flip) for step, flip in HOPS]

    pieces = []
    for j in range(2):
        got = [lax.dynamic_index_in_dim(obs, 8 * j + me, 1, keepdims=False)]
        for (step, flip), target in zip(HOPS, targets):
            part = lax.dynamic_index_in_dim(obs, 8 * j + target, 1, keepdims=False)
            got.append(across(part, step, flip))
        pieces.append(got)

    meta = jnp.concatenate([tile_count.reshape(1), (tile_list - base).reshape(-1)])
    meta = lax.all_gather(meta, "prow", axis=0)
    meta = meta[jnp.stack([me] + sources)]

    split = spectra.reshape(blocks, share, 2, 8, parts * windows)
    mine = lax.all_to_all(split, "prow", split_axis=3, concat_axis=0, tiled=False)
    mine = mine.transpose(3, 1, 0, 2, 4).reshape(2, blocks, width, parts * windows)
    values = mine.astype(jnp.float32)
    power = jnp.sum(values * values, axis=-1, keepdims=True) / windows
    white = (values * lax.rsqrt(power + EPS)).astype(jnp.bfloat16)

    outs = []
    reach = BAND - blocks
    near = along(white, -1)
    far = along(white[:, :reach], -2)
    for j in range(2):
        own_sum, near_sum, far_sum = tile_call(meta, pieces[j], white[j], near[j], far[j])
        near_got = along(near_sum, 1)
        far_got = along(far_sum, 2)
        grad = final_call(mine[j], own_sum, near_got, far_got)
        grad = grad.reshape(blocks, 8, share, parts * windows)
        outs.append(lax.all_to_all(grad, "prow", split_axis=1, concat_axis=0, tiled=False))
    whole = jnp.stack(outs).reshape(bins, blocks, share, parts, windows)
    return whole.transpose(1, 2, 0, 3, 4).astype(jnp.float32)


def solution(mesh):
    placed = (
        P("pcol", "prow", None, None, None),
        P("prow", "pcol", None, None),
        P("prow", "pcol"),
        P("prow", "pcol", None, None, None, None, None),
    )
    return jax.shard_map(
        local,
        mesh=mesh,
        in_specs=placed,
        out_specs=P("pcol", "prow", None, None, None),
        check_vma=False,
    )
```

```python
import functools

import jax
import jax.numpy as jnp
from jax import lax
from jax.experimental import pallas as pl
from jax.experimental.pallas import tpu as pltpu
from jax.sharding import PartitionSpec as P

BAND = 8
EPS = 1e-06
CURVE = 100.0
HOPS = ((1, 0), (3, 0), (1, 1), (3, 1), (0, 1), (2, 0), (2, 1))
STEPS = (1, 3, 2)
PLACES = (0, 2, 4, 3, 5, 1, 6, 7)
VMEM = pl.BlockSpec(memory_space=pltpu.VMEM)
SMEM = pl.BlockSpec(memory_space=pltpu.SMEM)
ANY = pl.BlockSpec(memory_space=pl.ANY)
HBM = pl.BlockSpec(memory_space=pltpu.HBM)
COPY_PARAMS = pltpu.CompilerParams(vmem_limit_bytes=55 * 1024 * 1024)
PARAMS = pltpu.CompilerParams(vmem_limit_bytes=40 * 1024 * 1024)


def setup_kernel(slots, meta, own, near, far, table0, table1, stack0, stack1, back0, back1):
    blocks, width, depth = own.shape[1:]
    reach = far.shape[1]
    span = blocks + reach + 1
    half = depth // 2
    for i in range(blocks * span):
        table0[i] = -1
        table1[i] = -1
    for k in range(8):

        def put(s, carry, k=k):
            a = meta[k, 1 + 2 * s]
            spot = a * span + meta[k, 2 + 2 * s] - a
            table0[spot] = k * slots + s
            table1[spot] = PLACES[k] * slots + s
            return carry

        lax.fori_loop(0, meta[k, 0], put, 0)
    for j, (stack, back) in enumerate(((stack0, back0), (stack1, back1))):
        for n in range(2 * blocks + reach):
            if n < blocks:
                block = own[j, n]
            elif n < 2 * blocks:
                block = near[j, n - blocks]
            else:
                block = far[j, n - 2 * blocks]
            turned = jnp.concatenate([block[:, half:], -block[:, :half]], axis=1)
            stack[n, :width] = block
            stack[n, width:] = turned
            if n < blocks:
                back[n, :width] = block
                back[n, width:] = -turned


def setup_call(slots, meta, own, near, far):
    blocks, width, depth = own.shape[1:]
    reach = far.shape[1]
    total = 2 * blocks + reach
    stack = jax.ShapeDtypeStruct((total, 2 * width, depth), own.dtype)
    back = jax.ShapeDtypeStruct((blocks, 2 * width, depth), own.dtype)
    return pl.pallas_call(
        functools.partial(setup_kernel, slots),
        out_shape=(
            jax.ShapeDtypeStruct((blocks * (blocks + reach + 1),), jnp.int32),
            jax.ShapeDtypeStruct((blocks * (blocks + reach + 1),), jnp.int32),
            stack,
            stack,
            back,
            back,
        ),
        in_specs=[SMEM, VMEM, VMEM, VMEM],
        out_specs=(SMEM, SMEM, VMEM, VMEM, VMEM, VMEM),
        compiler_params=PARAMS,
        name="setup",
    )(meta, own, near, far)


def slopes_of(table, held, upper, span, sums, b, low, high):
    width = upper.shape[0]
    pairs = []
    for a in range(low, high):
        spot = table[a * span + b - a]
        keep = spot >= 0
        spot = jnp.maximum(spot, 0)
        if a == high - 1:
            keep = jnp.logical_and(keep, jnp.logical_or(upper, a != b))
        halves = []
        for part in range(2):
            seen = held[spot, part].astype(jnp.float32) * width
            place = (a - low) * width
            diff = sums[place : place + width, part * width : (part + 1) * width] - seen
            slope = diff * lax.rsqrt(diff * diff * CURVE + float(width * width))
            halves.append(jnp.where(keep, slope, 0.0).astype(jnp.bfloat16))
        pairs.append(halves)
    return pairs


def products(back, block, low, high):
    width = back.shape[1] // 2
    rows = jnp.concatenate([back[a, :width] for a in range(low, high)], axis=0)
    return lax.dot_general(
        rows, block, (((1,), (1,)), ((), ())), preferred_element_type=jnp.float32
    )


def turned_product(slopes, back, a, first, last):
    left = jnp.concatenate([slopes[a, d] for d in range(first, last)], axis=1)
    return lax.dot_general(
        left, back[a], (((0,), (0,)), ((), ())), preferred_element_type=jnp.float32
    )


def upper_of(width):
    return lax.broadcasted_iota(jnp.int32, (width, width), 1) > lax.broadcasted_iota(
        jnp.int32, (width, width), 0
    )


def row_range(b, blocks, span):
    return max(0, b - span + 1), min(blocks, b + 1)


def side_kernel(start, table, held, stack, back, slopes, out, grad):
    blocks, double, depth = back.shape
    width = double // 2
    reach = stack.shape[0] - 2 * blocks
    span = blocks + reach + 1
    count = out.shape[0]
    upper = upper_of(width)
    grad[...] = jnp.zeros_like(grad)

    def column(b, low, high):
        sums = products(back, stack[b], low, high)
        pairs = slopes_of(table, held, upper, span, sums, b, low, high)
        for a in range(low, high):
            for part in range(2):
                slopes[a, b - start, part * width : (part + 1) * width] = pairs[a - low][part]

    def full(b, carry):
        column(b, 0, blocks)
        return carry

    stop = start + count
    lax.fori_loop(start, max(start, min(stop, span)), full, 0)
    for b in range(max(start, span), stop):
        column(b, *row_range(b, blocks, span))
    for a in range(blocks):
        last = min(stop, a + span)
        if last <= start:
            continue
        add = turned_product(slopes, back, a, 0, last - start)
        for b in range(start, last):
            grad[b - start] += add[(b - start) * width : (b - start + 1) * width]
    out[...] = grad[...].astype(jnp.bfloat16)


def nearby_kernel(table, held, stack, back, close, distant, grad, fresh):
    blocks, double, depth = back.shape
    width = double // 2
    total = stack.shape[0]
    reach = total - 2 * blocks
    span = blocks + reach + 1
    upper = upper_of(width)
    grad[...] = jnp.zeros_like(grad)

    def rows(b, low, high, wide):
        add = jnp.dot(jnp.concatenate(wide, axis=0), stack[b], preferred_element_type=jnp.float32)
        for a in range(low, high):
            grad[a] += add[(a - low) * width : (a - low + 1) * width]

    for b in range(blocks):
        sums = products(back, stack[b], 0, b + 1)
        pairs = slopes_of(table, held, upper, span, sums, b, 0, b + 1)
        for a in range(b + 1):
            for part in range(2):
                fresh[a, b - a, part * width : (part + 1) * width] = pairs[a][part]
        rows(b, 0, b + 1, [jnp.concatenate(pair, axis=1) for pair in pairs])

    def kept(slopes, a, n):
        return jnp.concatenate([slopes[a, n, :width], slopes[a, n, width:]], axis=1)

    def full(b, carry):
        rows(b, 0, blocks, [kept(close, a, b - blocks) for a in range(blocks)])
        return carry

    lax.fori_loop(blocks, span, full, 0)
    for b in range(span, total):
        low, high = row_range(b, blocks, span)
        slopes, first = (close, blocks) if b < 2 * blocks else (distant, 2 * blocks)
        rows(b, low, high, [kept(slopes, a, b - first) for a in range(low, high)])
    for a in range(blocks):
        add = turned_product(fresh, back, a, 0, blocks - a)
        for d in range(blocks - a):
            grad[a + d] += add[d * width : (d + 1) * width]


def cost(tiles, width, depth):
    return pl.CostEstimate(
        flops=tiles * 6 * width * depth * depth,
        bytes_accessed=tiles * 512 * 1024,
        transcendentals=0,
    )


def side_call(start, count, table, held, stack, back):
    blocks, double, depth = back.shape
    width = double // 2
    return pl.pallas_call(
        functools.partial(side_kernel, start),
        out_shape=(
            jax.ShapeDtypeStruct((blocks, count, double, width), jnp.bfloat16),
            jax.ShapeDtypeStruct((count, width, depth), jnp.bfloat16),
        ),
        in_specs=[SMEM] + [VMEM] * 3,
        out_specs=(VMEM, VMEM),
        scratch_shapes=[pltpu.VMEM((count, width, depth), jnp.float32)],
        compiler_params=PARAMS,
        cost_estimate=cost(4 * count, width, depth),
        name="side",
    )(table, held, stack, back)


def nearby_call(table, held, stack, back, close, distant):
    blocks, double, depth = back.shape
    width = double // 2
    return pl.pallas_call(
        nearby_kernel,
        out_shape=jax.ShapeDtypeStruct((blocks, width, depth), jnp.float32),
        in_specs=[SMEM] + [VMEM] * 5,
        out_specs=VMEM,
        scratch_shapes=[pltpu.VMEM((blocks, blocks, double, width), jnp.bfloat16)],
        compiler_params=PARAMS,
        cost_estimate=cost(20, width, depth),
        name="nearby",
    )(table, held, stack, back, close, distant)


def gather(pieces, held, sems):
    slots = pieces[0].shape[0]
    copies = [
        pltpu.make_async_copy(piece, held.at[pl.ds(k * slots, slots)], sems.at[k])
        for k, piece in enumerate(pieces)
    ]
    for copy in copies:
        copy.start()
    return copies


def collect_kernel(j, place, obs, pair, first, second, third, held, sems):
    slots = pair.shape[0]
    parts = [obs.at[:, j, place[0], place[1]], pair.at[:, place[0]], first, second, third]
    starts = [0, 1, 2, 4, 6]
    copies = [
        pltpu.make_async_copy(
            part, held.at[pl.ds(start * slots, part.shape[0])], sems.at[k]
        )
        for k, (part, start) in enumerate(zip(parts, starts))
    ]
    for copy in copies:
        copy.start()
    for copy in copies:
        copy.wait()


def collect_call(j, place, obs, pair, arrived):
    slots = pair.shape[0]
    return pl.pallas_call(
        functools.partial(collect_kernel, j),
        out_shape=jax.ShapeDtypeStruct((8 * slots,) + pair.shape[2:], pair.dtype),
        in_specs=[SMEM, HBM] + [ANY] * 4,
        out_specs=VMEM,
        scratch_shapes=[pltpu.SemaphoreType.DMA((5,))],
        compiler_params=PARAMS,
        name="collect",
    )(place, obs, pair, *arrived)


def swap_kernel(j, place, obs, out, sem):
    copy = pltpu.make_async_copy(obs.at[:, j, :, 1 - place[1]], out, sem)
    copy.start()
    copy.wait()


def swap_call(j, place, obs):
    slots, _, chips = obs.shape[:3]
    return pl.pallas_call(
        functools.partial(swap_kernel, j),
        out_shape=jax.ShapeDtypeStruct((slots, chips) + obs.shape[4:], obs.dtype),
        in_specs=[SMEM, HBM],
        out_specs=VMEM,
        scratch_shapes=[pltpu.SemaphoreType.DMA(())],
        compiler_params=COPY_PARAMS,
        name="swap",
    )(place, obs)


def pack_kernel(j, place, obs, pair, first, second, third, sems):
    chips = pair.shape[1]
    copies = []
    for k, (step, out) in enumerate(zip(STEPS, (first, second, third))):
        chip = lax.rem(place[0] + step, chips)
        copies.append((obs.at[:, j, chip, place[1]], out.at[pl.ds(0, out.shape[0] // 2)], 2 * k))
        copies.append((pair.at[:, chip], out.at[pl.ds(out.shape[0] // 2, out.shape[0] // 2)], 2 * k + 1))
    copies = [pltpu.make_async_copy(src, dst, sems.at[k]) for src, dst, k in copies]
    for copy in copies:
        copy.start()
    for copy in copies:
        copy.wait()


def pack_call(j, place, obs, pair):
    slots = pair.shape[0]
    out = jax.ShapeDtypeStruct((2 * slots,) + pair.shape[2:], pair.dtype)
    return pl.pallas_call(
        functools.partial(pack_kernel, j),
        out_shape=(out, out, out),
        in_specs=[SMEM, HBM, ANY],
        out_specs=(VMEM, VMEM, VMEM),
        scratch_shapes=[pltpu.SemaphoreType.DMA((6,))],
        compiler_params=COPY_PARAMS,
        name="pack",
    )(place, obs, pair)


def tile_kernel(table, *refs):
    stack, back, grad_own, grad_near, grad_far, held, slopes, grad, sems = refs[8:]
    blocks, double, _ = back.shape
    width = double // 2
    total = stack.shape[0]
    reach = total - 2 * blocks
    span = blocks + reach + 1
    copies = gather(refs[:8], held, sems)
    grad[...] = jnp.zeros_like(grad)
    upper = upper_of(width)
    for copy in copies:
        copy.wait()

    def column(b, low, high):
        pairs = slopes_of(
            table, held, upper, span, products(back, stack[b], low, high), b, low, high
        )
        wide = []
        for a in range(low, high):
            for part in range(2):
                slopes[a, b - a, part * width : (part + 1) * width] = pairs[a - low][part]
            wide.append(jnp.concatenate(pairs[a - low], axis=1))
        add = jnp.dot(jnp.concatenate(wide, axis=0), stack[b], preferred_element_type=jnp.float32)
        for a in range(low, high):
            grad[a] += add[(a - low) * width : (a - low + 1) * width]

    for b in range(blocks - 1):
        column(b, 0, b + 1)

    def full(b, carry):
        column(b, 0, blocks)
        return carry

    lax.fori_loop(blocks - 1, span, full, 0)
    for b in range(span, total):
        column(b, *row_range(b, blocks, span))

    def mirror(a, carry):
        add = turned_product(slopes, back, a, 0, span)
        for d in range(span):
            grad[a + d] += add[d * width : (d + 1) * width]
        return carry

    lax.fori_loop(0, blocks, mirror, 0)
    grad_own[...] = grad[:blocks]
    grad_near[...] = grad[blocks : 2 * blocks].astype(jnp.bfloat16)
    grad_far[...] = grad[2 * blocks :].astype(jnp.bfloat16)


def tile_call(table, pieces, stack, back):
    slots = pieces[0].shape[0]
    blocks, double, depth = back.shape
    width = double // 2
    total = stack.shape[0]
    reach = total - 2 * blocks
    span = blocks + reach + 1
    return pl.pallas_call(
        tile_kernel,
        out_shape=(
            jax.ShapeDtypeStruct((blocks, width, depth), jnp.float32),
            jax.ShapeDtypeStruct((blocks, width, depth), jnp.bfloat16),
            jax.ShapeDtypeStruct((reach, width, depth), jnp.bfloat16),
        ),
        in_specs=[SMEM] + [ANY] * 8 + [VMEM] * 2,
        out_specs=(VMEM, VMEM, VMEM),
        scratch_shapes=[
            pltpu.VMEM((8 * slots, 2, width, width), jnp.bfloat16),
            pltpu.VMEM((blocks, span, double, width), jnp.bfloat16),
            pltpu.VMEM((total, width, depth), jnp.float32),
            pltpu.SemaphoreType.DMA((8,)),
        ],
        compiler_params=PARAMS,
        cost_estimate=cost(0, width, depth),
        name="tiles",
    )(table, *pieces, stack, back)


def final_kernel(spectra, own0, near0, far0, own1, near1, far1, out):
    for j, (own, near, far) in enumerate(((own0, near0, far0), (own1, near1, far1))):
        blocks = own.shape[0]
        reach = far.shape[0]
        scale = 2.0 / spectra.shape[-1]
        for n in range(blocks):
            values = spectra[j, n].astype(jnp.float32)
            power = jnp.sum(values * values, axis=1, keepdims=True) * scale
            factor = lax.rsqrt(power + EPS)
            total = own[n] + near[n].astype(jnp.float32)
            if n < reach:
                total = total + far[n].astype(jnp.float32)
            inner = jnp.sum(total * values, axis=1, keepdims=True) * scale
            grad = factor * total - values * (factor * factor * factor * inner)
            share = grad.shape[0] // 8
            for r in range(8):
                out[r, j, n] = grad[r * share : (r + 1) * share].astype(jnp.bfloat16)


def final_call(spectra, sums0, sums1):
    _, blocks, width, depth = spectra.shape
    return pl.pallas_call(
        final_kernel,
        out_shape=jax.ShapeDtypeStruct((8, 2, blocks, width // 8, depth), jnp.bfloat16),
        in_specs=[VMEM] * 7,
        out_specs=VMEM,
        compiler_params=PARAMS,
        name="final",
    )(spectra, *sums0, *sums1)


def route_across(step, flip):
    chips = lax.axis_size("prow") // 2
    return "prow", [
        (2 * y + c, 2 * ((y + step) % chips) + (c ^ flip)) for y in range(chips) for c in range(2)
    ]


def route_along(distance):
    devices = range(lax.axis_size("pcol"))
    return "pcol", [(i - distance, i) for i in devices if i - distance in devices]


def send(values, route, after=None):
    if after is not None:
        values, _ = lax.optimization_barrier((values, after))
    return lax.ppermute(values, *route)


def local(spectra, tile_list, tile_count, observed):
    blocks, share, bins, parts, windows = spectra.shape
    slots = tile_list.shape[2]
    width = 8 * share
    depth = parts * windows
    reach = BAND - blocks
    me = lax.axis_index("prow")
    chip = me // 2
    core = me % 2
    base = lax.axis_index("pcol") * blocks
    targets = [(chip + step) % 4 * 2 + (core ^ flip) for step, flip in HOPS]
    lists = [me] + [(chip - step) % 4 * 2 + (core ^ flip) for step, flip in HOPS]
    routes = [route_across(*hop) for hop in HOPS]
    obs = observed[0, 0]

    meta = jnp.concatenate([tile_count.reshape(1), (tile_list - base).reshape(-1)])
    count = meta.shape[0]
    meta = jnp.pad(meta.astype(jnp.bfloat16).reshape(1, count), ((0, share - 1), (0, depth - count)))
    load = spectra.reshape(blocks, share, 2, 8, depth).transpose(3, 2, 0, 1, 4)
    load = load.reshape(8, 2 * blocks, share, depth)
    load = jnp.concatenate([load, jnp.broadcast_to(meta, (8, 1) + meta.shape)], axis=1)

    def cut(data, j, k):
        return lax.dynamic_index_in_dim(data, 8 * j + targets[k], 1, keepdims=False)

    early = [cut(obs, 0, k) for k in range(2)]
    early, load, obs = lax.optimization_barrier((early, load, obs))
    load = lax.all_to_all(load, "prow", split_axis=0, concat_axis=0, tiled=True)
    parts0 = early + [cut(obs, 0, k) for k in range(2, 4)]
    _, obs = lax.optimization_barrier((parts0[2:], obs))
    parts0 += [cut(obs, 0, k) for k in range(4, 7)]
    load, _ = lax.optimization_barrier((load, parts0))
    sent0 = [send(parts0[k], routes[k]) for k in range(4)]
    sent0.append(send(parts0[4], routes[4], sent0[0]))
    sent0.append(send(parts0[5], routes[5], sent0[0]))
    sent0.append(send(parts0[6], routes[6], sent0[1]))
    whole_obs = observed.reshape((slots, 2, 4, 2) + observed.shape[4:])
    place = jnp.stack([chip, core])
    place, _ = lax.optimization_barrier((place, parts0[2:4]))
    swapped = swap_call(1, place, whole_obs)
    load, swapped = lax.optimization_barrier((load, swapped))
    pair = send(swapped, route_across(0, 1), sent0[:4])
    meta = load[:, -1, 0, :count].astype(jnp.int32)[jnp.stack(lists)]
    mine = load[:, :-1].reshape(8, 2, blocks, share, depth)
    mine = mine.transpose(1, 2, 0, 3, 4).reshape(2, blocks, width, depth)
    values = mine.astype(jnp.float32)
    power = jnp.sum(values * values, axis=-1, keepdims=True) / windows
    white = (values * lax.rsqrt(power + EPS)).astype(jnp.bfloat16)
    near = send(white, route_along(-1))
    far = send(white[:, :reach], route_along(-2))
    packed = pack_call(1, place, whole_obs, pair)
    sent1 = [
        send(part, route_across(step, 0), after)
        for part, step, after in zip(packed, STEPS, ((near, sent0[5]), (far, sent0[6]), sent0[4]))
    ]
    table0, table1, stack0, stack1, back0, back1 = setup_call(slots, meta, white, near, far)

    own = lax.dynamic_index_in_dim(obs, me, 1, keepdims=False)
    own_sum, near_sum, far_sum = tile_call(table0, [own] + sent0, stack0, back0)
    sums0 = own_sum, send(near_sum, route_along(1)), send(far_sum, route_along(2))
    sent1, sums0 = lax.optimization_barrier((sent1, sums0))
    held = collect_call(1, place, whole_obs, pair, sent1)
    distant, far_sum = side_call(2 * blocks, reach, table1, held, stack1, back1)
    far_sum, held = lax.optimization_barrier((far_sum, held))
    far_sum = send(far_sum, route_along(2))
    close, near_sum = side_call(blocks, blocks, table1, held, stack1, back1)
    near_sum = send(near_sum, route_along(1))
    own_sum = nearby_call(table1, held, stack1, back1, close, distant)
    grad = final_call(mine, sums0, (own_sum, near_sum, far_sum))
    grad = lax.all_to_all(grad, "prow", split_axis=0, concat_axis=0, tiled=True)
    whole = grad.transpose(2, 3, 1, 0, 4).reshape(blocks, share, bins, parts, windows)
    return whole.astype(jnp.float32)


def solution(mesh):
    placed = (
        P("pcol", "prow", None, None, None),
        P("prow", "pcol", None, None),
        P("prow", "pcol"),
        P("prow", "pcol", None, None, None, None, None),
    )
    return jax.shard_map(
        local,
        mesh=mesh,
        in_specs=placed,
        out_specs=P("pcol", "prow", None, None, None),
        check_vma=False,
    )
```

```python
import functools

import jax
import jax.numpy as jnp
from jax import lax
from jax.experimental import pallas as pl
from jax.experimental.pallas import tpu as pltpu
from jax.sharding import PartitionSpec as P

BAND = 8
EPS = 1e-06
CURVE = 100.0
HOPS = ((1, 0), (3, 0), (1, 1), (3, 1), (0, 1), (2, 0), (2, 1))
STEPS = (1, 3, 2)
PLACES = (0, 2, 4, 3, 5, 1, 6, 7)
VMEM = pl.BlockSpec(memory_space=pltpu.VMEM)
SMEM = pl.BlockSpec(memory_space=pltpu.SMEM)
ANY = pl.BlockSpec(memory_space=pl.ANY)
HBM = pl.BlockSpec(memory_space=pltpu.HBM)
COPY_PARAMS = pltpu.CompilerParams(vmem_limit_bytes=55 * 1024 * 1024)
PARAMS = pltpu.CompilerParams(vmem_limit_bytes=40 * 1024 * 1024)


def setup_kernel(slots, meta, own, near, far, table0, table1, stack0, stack1, back0, back1):
    blocks, width, depth = own.shape[1:]
    reach = far.shape[1]
    span = blocks + reach + 1
    half = depth // 2
    for i in range(blocks * span):
        table0[i] = -1
        table1[i] = -1
    for k in range(8):

        def put(s, carry, k=k):
            a = meta[k, 1 + 2 * s]
            spot = a * span + meta[k, 2 + 2 * s] - a
            table0[spot] = k * slots + s
            table1[spot] = PLACES[k] * slots + s
            return carry

        lax.fori_loop(0, meta[k, 0], put, 0)
    for j, (stack, back) in enumerate(((stack0, back0), (stack1, back1))):
        for n in range(2 * blocks + reach):
            if n < blocks:
                block = own[j, n]
            elif n < 2 * blocks:
                block = near[j, n - blocks]
            else:
                block = far[j, n - 2 * blocks]
            turned = jnp.concatenate([block[:, half:], -block[:, :half]], axis=1)
            stack[n, :width] = block
            stack[n, width:] = turned
            if n < blocks:
                back[n, :width] = block
                back[n, width:] = -turned


def setup_call(slots, meta, own, near, far):
    blocks, width, depth = own.shape[1:]
    reach = far.shape[1]
    total = 2 * blocks + reach
    stack = jax.ShapeDtypeStruct((total, 2 * width, depth), own.dtype)
    back = jax.ShapeDtypeStruct((blocks, 2 * width, depth), own.dtype)
    return pl.pallas_call(
        functools.partial(setup_kernel, slots),
        out_shape=(
            jax.ShapeDtypeStruct((blocks * (blocks + reach + 1),), jnp.int32),
            jax.ShapeDtypeStruct((blocks * (blocks + reach + 1),), jnp.int32),
            stack,
            stack,
            back,
            back,
        ),
        in_specs=[SMEM, VMEM, VMEM, VMEM],
        out_specs=(SMEM, SMEM, VMEM, VMEM, VMEM, VMEM),
        compiler_params=PARAMS,
        name="setup",
    )(meta, own, near, far)


def slopes_of(table, held, upper, span, sums, b, low, high):
    width = upper.shape[0]
    pairs = []
    for a in range(low, high):
        spot = table[a * span + b - a]
        keep = spot >= 0
        spot = jnp.maximum(spot, 0)
        if a == high - 1:
            keep = jnp.logical_and(keep, jnp.logical_or(upper, a != b))
        halves = []
        for part in range(2):
            seen = held[spot, part].astype(jnp.float32) * width
            place = (a - low) * width
            diff = sums[place : place + width, part * width : (part + 1) * width] - seen
            slope = diff * lax.rsqrt(diff * diff * CURVE + float(width * width))
            halves.append(jnp.where(keep, slope, 0.0).astype(jnp.bfloat16))
        pairs.append(halves)
    return pairs


def products(back, block, low, high):
    width = back.shape[1] // 2
    rows = jnp.concatenate([back[a, :width] for a in range(low, high)], axis=0)
    return lax.dot_general(
        rows, block, (((1,), (1,)), ((), ())), preferred_element_type=jnp.float32
    )


def turned_product(slopes, back, a, first, last):
    left = jnp.concatenate([slopes[a, d] for d in range(first, last)], axis=1)
    return lax.dot_general(
        left, back[a], (((0,), (0,)), ((), ())), preferred_element_type=jnp.float32
    )


def upper_of(width):
    return lax.broadcasted_iota(jnp.int32, (width, width), 1) > lax.broadcasted_iota(
        jnp.int32, (width, width), 0
    )


def row_range(b, blocks, span):
    return max(0, b - span + 1), min(blocks, b + 1)


def side_kernel(start, table, held, stack, back, slopes, out, grad):
    blocks, double, depth = back.shape
    width = double // 2
    reach = stack.shape[0] - 2 * blocks
    span = blocks + reach + 1
    count = out.shape[0]
    upper = upper_of(width)
    grad[...] = jnp.zeros_like(grad)

    def column(b, low, high):
        sums = products(back, stack[b], low, high)
        pairs = slopes_of(table, held, upper, span, sums, b, low, high)
        for a in range(low, high):
            for part in range(2):
                slopes[a, b - start, part * width : (part + 1) * width] = pairs[a - low][part]

    def full(b, carry):
        column(b, 0, blocks)
        return carry

    stop = start + count
    lax.fori_loop(start, max(start, min(stop, span)), full, 0)
    for b in range(max(start, span), stop):
        column(b, *row_range(b, blocks, span))
    for a in range(blocks):
        last = min(stop, a + span)
        if last <= start:
            continue
        add = turned_product(slopes, back, a, 0, last - start)
        for b in range(start, last):
            grad[b - start] += add[(b - start) * width : (b - start + 1) * width]
    out[...] = grad[...].astype(jnp.bfloat16)


def nearby_kernel(table, held, stack, back, close, distant, grad, fresh):
    blocks, double, depth = back.shape
    width = double // 2
    total = stack.shape[0]
    reach = total - 2 * blocks
    span = blocks + reach + 1
    upper = upper_of(width)
    grad[...] = jnp.zeros_like(grad)

    def rows(b, low, high, wide):
        add = jnp.dot(jnp.concatenate(wide, axis=0), stack[b], preferred_element_type=jnp.float32)
        for a in range(low, high):
            grad[a] += add[(a - low) * width : (a - low + 1) * width]

    for b in range(blocks):
        sums = products(back, stack[b], 0, b + 1)
        pairs = slopes_of(table, held, upper, span, sums, b, 0, b + 1)
        for a in range(b + 1):
            for part in range(2):
                fresh[a, b - a, part * width : (part + 1) * width] = pairs[a][part]
        rows(b, 0, b + 1, [jnp.concatenate(pair, axis=1) for pair in pairs])

    def kept(slopes, a, n):
        return jnp.concatenate([slopes[a, n, :width], slopes[a, n, width:]], axis=1)

    def full(b, carry):
        rows(b, 0, blocks, [kept(close, a, b - blocks) for a in range(blocks)])
        return carry

    lax.fori_loop(blocks, span, full, 0)
    for b in range(span, total):
        low, high = row_range(b, blocks, span)
        slopes, first = (close, blocks) if b < 2 * blocks else (distant, 2 * blocks)
        rows(b, low, high, [kept(slopes, a, b - first) for a in range(low, high)])
    for a in range(blocks):
        add = turned_product(fresh, back, a, 0, blocks - a)
        for d in range(blocks - a):
            grad[a + d] += add[d * width : (d + 1) * width]


def cost(tiles, width, depth):
    return pl.CostEstimate(
        flops=tiles * 6 * width * depth * depth,
        bytes_accessed=tiles * 512 * 1024,
        transcendentals=0,
    )


def side_call(start, count, table, held, stack, back):
    blocks, double, depth = back.shape
    width = double // 2
    return pl.pallas_call(
        functools.partial(side_kernel, start),
        out_shape=(
            jax.ShapeDtypeStruct((blocks, count, double, width), jnp.bfloat16),
            jax.ShapeDtypeStruct((count, width, depth), jnp.bfloat16),
        ),
        in_specs=[SMEM] + [VMEM] * 3,
        out_specs=(VMEM, VMEM),
        scratch_shapes=[pltpu.VMEM((count, width, depth), jnp.float32)],
        compiler_params=PARAMS,
        cost_estimate=cost(0, width, depth),
        name="side",
    )(table, held, stack, back)


def nearby_call(table, held, stack, back, close, distant):
    blocks, double, depth = back.shape
    width = double // 2
    return pl.pallas_call(
        nearby_kernel,
        out_shape=jax.ShapeDtypeStruct((blocks, width, depth), jnp.float32),
        in_specs=[SMEM] + [VMEM] * 5,
        out_specs=VMEM,
        scratch_shapes=[pltpu.VMEM((blocks, blocks, double, width), jnp.bfloat16)],
        compiler_params=PARAMS,
        cost_estimate=cost(0, width, depth),
        name="nearby",
    )(table, held, stack, back, close, distant)


def gather(pieces, held, sems):
    slots = pieces[0].shape[0]
    copies = [
        pltpu.make_async_copy(piece, held.at[pl.ds(k * slots, slots)], sems.at[k])
        for k, piece in enumerate(pieces)
    ]
    for copy in copies:
        copy.start()
    return copies


def collect_kernel(j, place, obs, pair, first, second, third, held, sems):
    slots = pair.shape[0]
    parts = [obs.at[:, j, place[0], place[1]], pair.at[:, place[0]], first, second, third]
    starts = [0, 1, 2, 4, 6]
    copies = [
        pltpu.make_async_copy(
            part, held.at[pl.ds(start * slots, part.shape[0])], sems.at[k]
        )
        for k, (part, start) in enumerate(zip(parts, starts))
    ]
    for copy in copies:
        copy.start()
    for copy in copies:
        copy.wait()


def collect_call(j, place, obs, pair, arrived):
    slots = pair.shape[0]
    return pl.pallas_call(
        functools.partial(collect_kernel, j),
        out_shape=jax.ShapeDtypeStruct((8 * slots,) + pair.shape[2:], pair.dtype),
        in_specs=[SMEM, HBM] + [ANY] * 4,
        out_specs=VMEM,
        scratch_shapes=[pltpu.SemaphoreType.DMA((5,))],
        compiler_params=PARAMS,
        name="collect",
    )(place, obs, pair, *arrived)


def swap_kernel(j, place, obs, out, sem):
    copy = pltpu.make_async_copy(obs.at[:, j, :, 1 - place[1]], out, sem)
    copy.start()
    copy.wait()


def swap_call(j, place, obs):
    slots, _, chips = obs.shape[:3]
    return pl.pallas_call(
        functools.partial(swap_kernel, j),
        out_shape=jax.ShapeDtypeStruct((slots, chips) + obs.shape[4:], obs.dtype),
        in_specs=[SMEM, HBM],
        out_specs=VMEM,
        scratch_shapes=[pltpu.SemaphoreType.DMA(())],
        compiler_params=COPY_PARAMS,
        name="swap",
    )(place, obs)


def pack_kernel(j, place, obs, pair, first, second, third, sems):
    chips = pair.shape[1]
    copies = []
    for k, (step, out) in enumerate(zip(STEPS, (first, second, third))):
        chip = lax.rem(place[0] + step, chips)
        copies.append((obs.at[:, j, chip, place[1]], out.at[pl.ds(0, out.shape[0] // 2)], 2 * k))
        copies.append((pair.at[:, chip], out.at[pl.ds(out.shape[0] // 2, out.shape[0] // 2)], 2 * k + 1))
    copies = [pltpu.make_async_copy(src, dst, sems.at[k]) for src, dst, k in copies]
    for copy in copies:
        copy.start()
    for copy in copies:
        copy.wait()


def pack_call(j, place, obs, pair):
    slots = pair.shape[0]
    out = jax.ShapeDtypeStruct((2 * slots,) + pair.shape[2:], pair.dtype)
    return pl.pallas_call(
        functools.partial(pack_kernel, j),
        out_shape=(out, out, out),
        in_specs=[SMEM, HBM, ANY],
        out_specs=(VMEM, VMEM, VMEM),
        scratch_shapes=[pltpu.SemaphoreType.DMA((6,))],
        compiler_params=COPY_PARAMS,
        name="pack",
    )(place, obs, pair)


def tile_kernel(table, *refs):
    stack, back, grad_own, grad_near, grad_far, held, slopes, grad, sems = refs[8:]
    blocks, double, _ = back.shape
    width = double // 2
    total = stack.shape[0]
    reach = total - 2 * blocks
    span = blocks + reach + 1
    copies = gather(refs[:8], held, sems)
    grad[...] = jnp.zeros_like(grad)
    upper = upper_of(width)
    for copy in copies:
        copy.wait()

    def column(b, low, high):
        pairs = slopes_of(
            table, held, upper, span, products(back, stack[b], low, high), b, low, high
        )
        wide = []
        for a in range(low, high):
            for part in range(2):
                slopes[a, b - a, part * width : (part + 1) * width] = pairs[a - low][part]
            wide.append(jnp.concatenate(pairs[a - low], axis=1))
        add = jnp.dot(jnp.concatenate(wide, axis=0), stack[b], preferred_element_type=jnp.float32)
        for a in range(low, high):
            grad[a] += add[(a - low) * width : (a - low + 1) * width]

    for b in range(blocks - 1):
        column(b, 0, b + 1)

    def full(b, carry):
        column(b, 0, blocks)
        return carry

    lax.fori_loop(blocks - 1, span, full, 0)
    for b in range(span, total):
        column(b, *row_range(b, blocks, span))

    def mirror(a, carry):
        add = turned_product(slopes, back, a, 0, span)
        for d in range(span):
            grad[a + d] += add[d * width : (d + 1) * width]
        return carry

    lax.fori_loop(0, blocks, mirror, 0)
    grad_own[...] = grad[:blocks]
    grad_near[...] = grad[blocks : 2 * blocks].astype(jnp.bfloat16)
    grad_far[...] = grad[2 * blocks :].astype(jnp.bfloat16)


def tile_call(table, pieces, stack, back):
    slots = pieces[0].shape[0]
    blocks, double, depth = back.shape
    width = double // 2
    total = stack.shape[0]
    reach = total - 2 * blocks
    span = blocks + reach + 1
    return pl.pallas_call(
        tile_kernel,
        out_shape=(
            jax.ShapeDtypeStruct((blocks, width, depth), jnp.float32),
            jax.ShapeDtypeStruct((blocks, width, depth), jnp.bfloat16),
            jax.ShapeDtypeStruct((reach, width, depth), jnp.bfloat16),
        ),
        in_specs=[SMEM] + [ANY] * 8 + [VMEM] * 2,
        out_specs=(VMEM, VMEM, VMEM),
        scratch_shapes=[
            pltpu.VMEM((8 * slots, 2, width, width), jnp.bfloat16),
            pltpu.VMEM((blocks, span, double, width), jnp.bfloat16),
            pltpu.VMEM((total, width, depth), jnp.float32),
            pltpu.SemaphoreType.DMA((8,)),
        ],
        compiler_params=PARAMS,
        cost_estimate=cost(0, width, depth),
        name="tiles",
    )(table, *pieces, stack, back)


def final_kernel(spectra, own0, near0, far0, own1, near1, far1, out):
    for j, (own, near, far) in enumerate(((own0, near0, far0), (own1, near1, far1))):
        blocks = own.shape[0]
        reach = far.shape[0]
        scale = 2.0 / spectra.shape[-1]
        for n in range(blocks):
            values = spectra[j, n].astype(jnp.float32)
            power = jnp.sum(values * values, axis=1, keepdims=True) * scale
            factor = lax.rsqrt(power + EPS)
            total = own[n] + near[n].astype(jnp.float32)
            if n < reach:
                total = total + far[n].astype(jnp.float32)
            inner = jnp.sum(total * values, axis=1, keepdims=True) * scale
            grad = factor * total - values * (factor * factor * factor * inner)
            share = grad.shape[0] // 8
            for r in range(8):
                out[r, j, n] = grad[r * share : (r + 1) * share].astype(jnp.bfloat16)


def final_call(spectra, sums0, sums1):
    _, blocks, width, depth = spectra.shape
    return pl.pallas_call(
        final_kernel,
        out_shape=jax.ShapeDtypeStruct((8, 2, blocks, width // 8, depth), jnp.bfloat16),
        in_specs=[VMEM] * 7,
        out_specs=VMEM,
        compiler_params=PARAMS,
        name="final",
    )(spectra, *sums0, *sums1)


def route_across(step, flip):
    chips = lax.axis_size("prow") // 2
    return "prow", [
        (2 * y + c, 2 * ((y + step) % chips) + (c ^ flip)) for y in range(chips) for c in range(2)
    ]


def route_along(distance):
    devices = range(lax.axis_size("pcol"))
    return "pcol", [(i - distance, i) for i in devices if i - distance in devices]


def send(values, route, after=None):
    if after is not None:
        values, _ = lax.optimization_barrier((values, after))
    return lax.ppermute(values, *route)


def local(spectra, tile_list, tile_count, observed):
    blocks, share, bins, parts, windows = spectra.shape
    slots = tile_list.shape[2]
    width = 8 * share
    depth = parts * windows
    reach = BAND - blocks
    me = lax.axis_index("prow")
    chip = me // 2
    core = me % 2
    base = lax.axis_index("pcol") * blocks
    targets = [(chip + step) % 4 * 2 + (core ^ flip) for step, flip in HOPS]
    lists = [me] + [(chip - step) % 4 * 2 + (core ^ flip) for step, flip in HOPS]
    routes = [route_across(*hop) for hop in HOPS]
    obs = observed[0, 0]

    def cut(data, j, k):
        return lax.dynamic_index_in_dim(data, 8 * j + targets[k], 1, keepdims=False)

    early = [cut(obs, 0, k) for k in range(2)]
    early, spectra, obs = lax.optimization_barrier((early, spectra, obs))
    meta = jnp.concatenate([tile_count.reshape(1), (tile_list - base).reshape(-1)])
    count = meta.shape[0]
    meta = jnp.pad(meta.astype(jnp.bfloat16).reshape(1, count), ((0, share - 1), (0, depth - count)))
    load = spectra.reshape(blocks, share, 2, 8, depth).transpose(3, 2, 0, 1, 4)
    load = load.reshape(8, 2 * blocks, share, depth)
    load = jnp.concatenate([load, jnp.broadcast_to(meta, (8, 1) + meta.shape)], axis=1)

    load = lax.all_to_all(load, "prow", split_axis=0, concat_axis=0, tiled=True)
    parts0 = early + [cut(obs, 0, k) for k in range(2, 4)]
    _, obs = lax.optimization_barrier((parts0[2:], obs))
    parts0 += [cut(obs, 0, k) for k in range(4, 7)]
    load, _ = lax.optimization_barrier((load, parts0))
    sent0 = [send(parts0[k], routes[k]) for k in range(4)]
    sent0.append(send(parts0[4], routes[4], sent0[0]))
    sent0.append(send(parts0[5], routes[5], sent0[0]))
    sent0.append(send(parts0[6], routes[6], sent0[1]))
    whole_obs = observed.reshape((slots, 2, 4, 2) + observed.shape[4:])
    place = jnp.stack([chip, core])
    place, _ = lax.optimization_barrier((place, parts0[2:4]))
    swapped = swap_call(1, place, whole_obs)
    load, swapped = lax.optimization_barrier((load, swapped))
    pair = send(swapped, route_across(0, 1), sent0[:4])
    meta = load[:, -1, 0, :count].astype(jnp.int32)[jnp.stack(lists)]
    mine = load[:, :-1].reshape(8, 2, blocks, share, depth)
    mine = mine.transpose(1, 2, 0, 3, 4).reshape(2, blocks, width, depth)
    values = mine.astype(jnp.float32)
    power = jnp.sum(values * values, axis=-1, keepdims=True) / windows
    white = (values * lax.rsqrt(power + EPS)).astype(jnp.bfloat16)
    near = send(white, route_along(-1))
    far = send(white[:, :reach], route_along(-2))
    packed = pack_call(1, place, whole_obs, pair)
    sent1 = [
        send(part, route_across(step, 0), after)
        for part, step, after in zip(packed, STEPS, ((near, sent0[5]), (far, sent0[6]), sent0[4]))
    ]
    table0, table1, stack0, stack1, back0, back1 = setup_call(slots, meta, white, near, far)

    own = lax.dynamic_index_in_dim(obs, me, 1, keepdims=False)
    own_sum, near_sum, far_sum = tile_call(table0, [own] + sent0, stack0, back0)
    sums0 = own_sum, send(near_sum, route_along(1)), send(far_sum, route_along(2))
    sent1, sums0 = lax.optimization_barrier((sent1, sums0))
    held = collect_call(1, place, whole_obs, pair, sent1)
    distant, far_sum = side_call(2 * blocks, reach, table1, held, stack1, back1)
    far_sum, held = lax.optimization_barrier((far_sum, held))
    far_sum = send(far_sum, route_along(2))
    close, near_sum = side_call(blocks, blocks, table1, held, stack1, back1)
    near_sum = send(near_sum, route_along(1))
    own_sum = nearby_call(table1, held, stack1, back1, close, distant)
    grad = final_call(mine, sums0, (own_sum, near_sum, far_sum))
    grad = lax.all_to_all(grad, "prow", split_axis=0, concat_axis=0, tiled=True)
    whole = grad.transpose(2, 3, 1, 0, 4).reshape(blocks, share, bins, parts, windows)
    return whole.astype(jnp.float32)


def solution(mesh):
    placed = (
        P("pcol", "prow", None, None, None),
        P("prow", "pcol", None, None),
        P("prow", "pcol"),
        P("prow", "pcol", None, None, None, None, None),
    )
    return jax.shard_map(
        local,
        mesh=mesh,
        in_specs=placed,
        out_specs=P("pcol", "prow", None, None, None),
        check_vma=False,
    )
```

```python
import functools

import jax
import jax.numpy as jnp
from jax import lax
from jax.experimental import pallas as pl
from jax.experimental.pallas import tpu as pltpu
from jax.sharding import PartitionSpec as P

BAND = 8
EPS = 1e-06
CURVE = 100.0
HOPS = ((1, 0), (3, 0), (1, 1), (3, 1), (0, 1), (2, 0), (2, 1))
STEPS = (1, 3, 2)
PLACES = (0, 2, 4, 3, 5, 1, 6, 7)
VMEM = pl.BlockSpec(memory_space=pltpu.VMEM)
SMEM = pl.BlockSpec(memory_space=pltpu.SMEM)
ANY = pl.BlockSpec(memory_space=pl.ANY)
HBM = pl.BlockSpec(memory_space=pltpu.HBM)
COPY_PARAMS = pltpu.CompilerParams(vmem_limit_bytes=55 * 1024 * 1024)
PARAMS = pltpu.CompilerParams(vmem_limit_bytes=40 * 1024 * 1024)


def setup_kernel(slots, meta, own, near, far, table0, table1, stack0, stack1, back0, back1):
    blocks, width, depth = own.shape[1:]
    reach = far.shape[1]
    span = blocks + reach + 1
    half = depth // 2
    for i in range(blocks * span):
        table0[i] = -1
        table1[i] = -1
    for k in range(8):

        def put(s, carry, k=k):
            a = meta[k, 1 + 2 * s]
            spot = a * span + meta[k, 2 + 2 * s] - a
            table0[spot] = k * slots + s
            table1[spot] = PLACES[k] * slots + s
            return carry

        lax.fori_loop(0, meta[k, 0], put, 0)
    for j, (stack, back) in enumerate(((stack0, back0), (stack1, back1))):
        for n in range(2 * blocks + reach):
            if n < blocks:
                block = own[j, n]
            elif n < 2 * blocks:
                block = near[j, n - blocks]
            else:
                block = far[j, n - 2 * blocks]
            turned = jnp.concatenate([block[:, half:], -block[:, :half]], axis=1)
            stack[n, :width] = block
            stack[n, width:] = turned
            if n < blocks:
                back[n, :width] = block
                back[n, width:] = -turned


def setup_call(slots, meta, own, near, far):
    blocks, width, depth = own.shape[1:]
    reach = far.shape[1]
    total = 2 * blocks + reach
    stack = jax.ShapeDtypeStruct((total, 2 * width, depth), own.dtype)
    back = jax.ShapeDtypeStruct((blocks, 2 * width, depth), own.dtype)
    return pl.pallas_call(
        functools.partial(setup_kernel, slots),
        out_shape=(
            jax.ShapeDtypeStruct((blocks * (blocks + reach + 1),), jnp.int32),
            jax.ShapeDtypeStruct((blocks * (blocks + reach + 1),), jnp.int32),
            stack,
            stack,
            back,
            back,
        ),
        in_specs=[SMEM, VMEM, VMEM, VMEM],
        out_specs=(SMEM, SMEM, VMEM, VMEM, VMEM, VMEM),
        compiler_params=PARAMS,
        name="setup",
    )(meta, own, near, far)


def slopes_of(table, held, upper, span, sums, b, low, high):
    width = upper.shape[0]
    pairs = []
    for a in range(low, high):
        spot = table[a * span + b - a]
        keep = spot >= 0
        spot = jnp.maximum(spot, 0)
        if a == high - 1:
            keep = jnp.logical_and(keep, jnp.logical_or(upper, a != b))
        halves = []
        for part in range(2):
            seen = held[spot, part].astype(jnp.float32) * width
            place = (a - low) * width
            diff = sums[place : place + width, part * width : (part + 1) * width] - seen
            slope = diff * lax.rsqrt(diff * diff * CURVE + float(width * width))
            halves.append(jnp.where(keep, slope, 0.0).astype(jnp.bfloat16))
        pairs.append(halves)
    return pairs


def products(back, block, low, high):
    width = back.shape[1] // 2
    rows = jnp.concatenate([back[a, :width] for a in range(low, high)], axis=0)
    return lax.dot_general(
        rows, block, (((1,), (1,)), ((), ())), preferred_element_type=jnp.float32
    )


def turned_product(slopes, back, a, first, last):
    left = jnp.concatenate([slopes[a, d] for d in range(first, last)], axis=1)
    return lax.dot_general(
        left, back[a], (((0,), (0,)), ((), ())), preferred_element_type=jnp.float32
    )


def upper_of(width):
    return lax.broadcasted_iota(jnp.int32, (width, width), 1) > lax.broadcasted_iota(
        jnp.int32, (width, width), 0
    )


def row_range(b, blocks, span):
    return max(0, b - span + 1), min(blocks, b + 1)


def side_kernel(start, table, held, stack, back, slopes, out, grad):
    blocks, double, depth = back.shape
    width = double // 2
    reach = stack.shape[0] - 2 * blocks
    span = blocks + reach + 1
    count = out.shape[0]
    upper = upper_of(width)
    grad[...] = jnp.zeros_like(grad)

    def column(b, low, high):
        sums = products(back, stack[b], low, high)
        pairs = slopes_of(table, held, upper, span, sums, b, low, high)
        for a in range(low, high):
            for part in range(2):
                slopes[a, b - start, part * width : (part + 1) * width] = pairs[a - low][part]

    def full(b, carry):
        column(b, 0, blocks)
        return carry

    stop = start + count
    lax.fori_loop(start, max(start, min(stop, span)), full, 0)
    for b in range(max(start, span), stop):
        column(b, *row_range(b, blocks, span))
    for a in range(blocks):
        last = min(stop, a + span)
        if last <= start:
            continue
        add = turned_product(slopes, back, a, 0, last - start)
        for b in range(start, last):
            grad[b - start] += add[(b - start) * width : (b - start + 1) * width]
    out[...] = grad[...].astype(jnp.bfloat16)


def nearby_kernel(table, held, stack, back, close, distant, grad, fresh):
    blocks, double, depth = back.shape
    width = double // 2
    total = stack.shape[0]
    reach = total - 2 * blocks
    span = blocks + reach + 1
    upper = upper_of(width)
    grad[...] = jnp.zeros_like(grad)

    def rows(b, low, high, wide):
        add = jnp.dot(jnp.concatenate(wide, axis=0), stack[b], preferred_element_type=jnp.float32)
        for a in range(low, high):
            grad[a] += add[(a - low) * width : (a - low + 1) * width]

    for b in range(blocks):
        sums = products(back, stack[b], 0, b + 1)
        pairs = slopes_of(table, held, upper, span, sums, b, 0, b + 1)
        for a in range(b + 1):
            for part in range(2):
                fresh[a, b - a, part * width : (part + 1) * width] = pairs[a][part]
        rows(b, 0, b + 1, [jnp.concatenate(pair, axis=1) for pair in pairs])

    def kept(slopes, a, n):
        return jnp.concatenate([slopes[a, n, :width], slopes[a, n, width:]], axis=1)

    def full(b, carry):
        rows(b, 0, blocks, [kept(close, a, b - blocks) for a in range(blocks)])
        return carry

    lax.fori_loop(blocks, span, full, 0)
    for b in range(span, total):
        low, high = row_range(b, blocks, span)
        slopes, first = (close, blocks) if b < 2 * blocks else (distant, 2 * blocks)
        rows(b, low, high, [kept(slopes, a, b - first) for a in range(low, high)])
    for a in range(blocks):
        add = turned_product(fresh, back, a, 0, blocks - a)
        for d in range(blocks - a):
            grad[a + d] += add[d * width : (d + 1) * width]


def cost(tiles, width, depth):
    return pl.CostEstimate(
        flops=tiles * 6 * width * depth * depth,
        bytes_accessed=tiles * 512 * 1024,
        transcendentals=0,
    )


def side_call(start, count, table, held, stack, back):
    blocks, double, depth = back.shape
    width = double // 2
    return pl.pallas_call(
        functools.partial(side_kernel, start),
        out_shape=(
            jax.ShapeDtypeStruct((blocks, count, double, width), jnp.bfloat16),
            jax.ShapeDtypeStruct((count, width, depth), jnp.bfloat16),
        ),
        in_specs=[SMEM] + [VMEM] * 3,
        out_specs=(VMEM, VMEM),
        scratch_shapes=[pltpu.VMEM((count, width, depth), jnp.float32)],
        compiler_params=PARAMS,
        cost_estimate=cost(0, width, depth),
        name="side",
    )(table, held, stack, back)


def nearby_call(table, held, stack, back, close, distant):
    blocks, double, depth = back.shape
    width = double // 2
    return pl.pallas_call(
        nearby_kernel,
        out_shape=jax.ShapeDtypeStruct((blocks, width, depth), jnp.float32),
        in_specs=[SMEM] + [VMEM] * 5,
        out_specs=VMEM,
        scratch_shapes=[pltpu.VMEM((blocks, blocks, double, width), jnp.bfloat16)],
        compiler_params=PARAMS,
        cost_estimate=cost(0, width, depth),
        name="nearby",
    )(table, held, stack, back, close, distant)


def gather(pieces, held, sems):
    slots = pieces[0].shape[0]
    copies = [
        pltpu.make_async_copy(piece, held.at[pl.ds(k * slots, slots)], sems.at[k])
        for k, piece in enumerate(pieces)
    ]
    for copy in copies:
        copy.start()
    return copies


def collect_kernel(j, place, obs, pair, first, second, third, held, sems):
    slots = pair.shape[0]
    parts = [obs.at[:, j, place[0], place[1]], pair.at[:, place[0]], first, second, third]
    starts = [0, 1, 2, 4, 6]
    copies = [
        pltpu.make_async_copy(
            part, held.at[pl.ds(start * slots, part.shape[0])], sems.at[k]
        )
        for k, (part, start) in enumerate(zip(parts, starts))
    ]
    for copy in copies:
        copy.start()
    for copy in copies:
        copy.wait()


def collect_call(j, place, obs, pair, arrived):
    slots = pair.shape[0]
    return pl.pallas_call(
        functools.partial(collect_kernel, j),
        out_shape=jax.ShapeDtypeStruct((8 * slots,) + pair.shape[2:], pair.dtype),
        in_specs=[SMEM, HBM] + [ANY] * 4,
        out_specs=VMEM,
        scratch_shapes=[pltpu.SemaphoreType.DMA((5,))],
        compiler_params=PARAMS,
        name="collect",
    )(place, obs, pair, *arrived)


def swap_kernel(j, place, obs, out, sem):
    copy = pltpu.make_async_copy(obs.at[:, j, :, 1 - place[1]], out, sem)
    copy.start()
    copy.wait()


def swap_call(j, place, obs):
    slots, _, chips = obs.shape[:3]
    return pl.pallas_call(
        functools.partial(swap_kernel, j),
        out_shape=jax.ShapeDtypeStruct((slots, chips) + obs.shape[4:], obs.dtype),
        in_specs=[SMEM, HBM],
        out_specs=VMEM,
        scratch_shapes=[pltpu.SemaphoreType.DMA(())],
        compiler_params=COPY_PARAMS,
        name="swap",
    )(place, obs)


def pack_kernel(j, place, obs, pair, first, second, third, sems):
    chips = pair.shape[1]
    copies = []
    for k, (step, out) in enumerate(zip(STEPS, (first, second, third))):
        chip = lax.rem(place[0] + step, chips)
        copies.append((obs.at[:, j, chip, place[1]], out.at[pl.ds(0, out.shape[0] // 2)], 2 * k))
        copies.append((pair.at[:, chip], out.at[pl.ds(out.shape[0] // 2, out.shape[0] // 2)], 2 * k + 1))
    copies = [pltpu.make_async_copy(src, dst, sems.at[k]) for src, dst, k in copies]
    for copy in copies:
        copy.start()
    for copy in copies:
        copy.wait()


def pack_call(j, place, obs, pair):
    slots = pair.shape[0]
    out = jax.ShapeDtypeStruct((2 * slots,) + pair.shape[2:], pair.dtype)
    return pl.pallas_call(
        functools.partial(pack_kernel, j),
        out_shape=(out, out, out),
        in_specs=[SMEM, HBM, ANY],
        out_specs=(VMEM, VMEM, VMEM),
        scratch_shapes=[pltpu.SemaphoreType.DMA((6,))],
        compiler_params=COPY_PARAMS,
        name="pack",
    )(place, obs, pair)


def tile_kernel(table, *refs):
    stack, back, grad_own, grad_near, grad_far, held, slopes, grad, sems = refs[8:]
    blocks, double, _ = back.shape
    width = double // 2
    total = stack.shape[0]
    reach = total - 2 * blocks
    span = blocks + reach + 1
    copies = gather(refs[:8], held, sems)
    grad[...] = jnp.zeros_like(grad)
    upper = upper_of(width)
    for copy in copies:
        copy.wait()

    def column(b, low, high):
        pairs = slopes_of(
            table, held, upper, span, products(back, stack[b], low, high), b, low, high
        )
        wide = []
        for a in range(low, high):
            for part in range(2):
                slopes[a, b - a, part * width : (part + 1) * width] = pairs[a - low][part]
            wide.append(jnp.concatenate(pairs[a - low], axis=1))
        add = jnp.dot(jnp.concatenate(wide, axis=0), stack[b], preferred_element_type=jnp.float32)
        for a in range(low, high):
            grad[a] += add[(a - low) * width : (a - low + 1) * width]

    for b in range(blocks - 1):
        column(b, 0, b + 1)

    def full(b, carry):
        column(b, 0, blocks)
        return carry

    lax.fori_loop(blocks - 1, span, full, 0)
    for b in range(span, total):
        column(b, *row_range(b, blocks, span))

    def mirror(a, carry):
        add = turned_product(slopes, back, a, 0, span)
        for d in range(span):
            grad[a + d] += add[d * width : (d + 1) * width]
        return carry

    lax.fori_loop(0, blocks, mirror, 0)
    grad_own[...] = grad[:blocks]
    grad_near[...] = grad[blocks : 2 * blocks].astype(jnp.bfloat16)
    grad_far[...] = grad[2 * blocks :].astype(jnp.bfloat16)


def tile_call(table, pieces, stack, back):
    slots = pieces[0].shape[0]
    blocks, double, depth = back.shape
    width = double // 2
    total = stack.shape[0]
    reach = total - 2 * blocks
    span = blocks + reach + 1
    return pl.pallas_call(
        tile_kernel,
        out_shape=(
            jax.ShapeDtypeStruct((blocks, width, depth), jnp.float32),
            jax.ShapeDtypeStruct((blocks, width, depth), jnp.bfloat16),
            jax.ShapeDtypeStruct((reach, width, depth), jnp.bfloat16),
        ),
        in_specs=[SMEM] + [ANY] * 8 + [VMEM] * 2,
        out_specs=(VMEM, VMEM, VMEM),
        scratch_shapes=[
            pltpu.VMEM((8 * slots, 2, width, width), jnp.bfloat16),
            pltpu.VMEM((blocks, span, double, width), jnp.bfloat16),
            pltpu.VMEM((total, width, depth), jnp.float32),
            pltpu.SemaphoreType.DMA((8,)),
        ],
        compiler_params=PARAMS,
        cost_estimate=cost(0, width, depth),
        name="tiles",
    )(table, *pieces, stack, back)


def final_kernel(spectra, own0, near0, far0, own1, near1, far1, out):
    for j, (own, near, far) in enumerate(((own0, near0, far0), (own1, near1, far1))):
        blocks = own.shape[0]
        reach = far.shape[0]
        scale = 2.0 / spectra.shape[-1]
        for n in range(blocks):
            values = spectra[j, n].astype(jnp.float32)
            power = jnp.sum(values * values, axis=1, keepdims=True) * scale
            factor = lax.rsqrt(power + EPS)
            total = own[n] + near[n].astype(jnp.float32)
            if n < reach:
                total = total + far[n].astype(jnp.float32)
            inner = jnp.sum(total * values, axis=1, keepdims=True) * scale
            grad = factor * total - values * (factor * factor * factor * inner)
            share = grad.shape[0] // 8
            for r in range(8):
                out[r, j, n] = grad[r * share : (r + 1) * share].astype(jnp.bfloat16)


def final_call(spectra, sums0, sums1):
    _, blocks, width, depth = spectra.shape
    return pl.pallas_call(
        final_kernel,
        out_shape=jax.ShapeDtypeStruct((8, 2, blocks, width // 8, depth), jnp.bfloat16),
        in_specs=[VMEM] * 7,
        out_specs=VMEM,
        compiler_params=PARAMS,
        name="final",
    )(spectra, *sums0, *sums1)


def route_across(step, flip):
    chips = lax.axis_size("prow") // 2
    return "prow", [
        (2 * y + c, 2 * ((y + step) % chips) + (c ^ flip)) for y in range(chips) for c in range(2)
    ]


def route_along(distance):
    devices = range(lax.axis_size("pcol"))
    return "pcol", [(i - distance, i) for i in devices if i - distance in devices]


def send(values, route, after=None):
    if after is not None:
        values, _ = lax.optimization_barrier((values, after))
    return lax.ppermute(values, *route)


def local(spectra, tile_list, tile_count, observed):
    blocks, share, bins, parts, windows = spectra.shape
    slots = tile_list.shape[2]
    width = 8 * share
    depth = parts * windows
    reach = BAND - blocks
    me = lax.axis_index("prow")
    chip = me // 2
    core = me % 2
    base = lax.axis_index("pcol") * blocks
    targets = [(chip + step) % 4 * 2 + (core ^ flip) for step, flip in HOPS]
    lists = [me] + [(chip - step) % 4 * 2 + (core ^ flip) for step, flip in HOPS]
    routes = [route_across(*hop) for hop in HOPS]
    obs = observed[0, 0]

    def cut(data, j, k):
        return lax.dynamic_index_in_dim(data, 8 * j + targets[k], 1, keepdims=False)

    early = [cut(obs, 0, 0)]
    _, obs = lax.optimization_barrier((early, obs))
    early.append(cut(obs, 0, 1))
    _, spectra, obs = lax.optimization_barrier((early, spectra, obs))
    meta = jnp.concatenate([tile_count.reshape(1), (tile_list - base).reshape(-1)])
    count = meta.shape[0]
    meta = jnp.pad(meta.astype(jnp.bfloat16).reshape(1, count), ((0, share - 1), (0, depth - count)))
    load = spectra.reshape(blocks, share, 2, 8, depth).transpose(3, 2, 0, 1, 4)
    load = load.reshape(8, 2 * blocks, share, depth)
    load = jnp.concatenate([load, jnp.broadcast_to(meta, (8, 1) + meta.shape)], axis=1)

    load = lax.all_to_all(load, "prow", split_axis=0, concat_axis=0, tiled=True)
    parts0 = early + [cut(obs, 0, k) for k in range(2, 4)]
    _, obs = lax.optimization_barrier((parts0[2:], obs))
    parts0 += [cut(obs, 0, k) for k in range(4, 7)]
    load, _ = lax.optimization_barrier((load, parts0))
    sent0 = [send(parts0[k], routes[k]) for k in range(4)]
    sent0.append(send(parts0[4], routes[4], sent0[0]))
    sent0.append(send(parts0[5], routes[5], sent0[0]))
    sent0.append(send(parts0[6], routes[6], sent0[1]))
    whole_obs = observed.reshape((slots, 2, 4, 2) + observed.shape[4:])
    place = jnp.stack([chip, core])
    place, _ = lax.optimization_barrier((place, parts0[2:4]))
    swapped = swap_call(1, place, whole_obs)
    load, swapped = lax.optimization_barrier((load, swapped))
    pair = send(swapped, route_across(0, 1), sent0[:4])
    meta = load[:, -1, 0, :count].astype(jnp.int32)[jnp.stack(lists)]
    mine = load[:, :-1].reshape(8, 2, blocks, share, depth)
    mine = mine.transpose(1, 2, 0, 3, 4).reshape(2, blocks, width, depth)
    values = mine.astype(jnp.float32)
    power = jnp.sum(values * values, axis=-1, keepdims=True) / windows
    white = (values * lax.rsqrt(power + EPS)).astype(jnp.bfloat16)
    near = send(white, route_along(-1))
    far = send(white[:, :reach], route_along(-2))
    packed = pack_call(1, place, whole_obs, pair)
    sent1 = [
        send(part, route_across(step, 0), after)
        for part, step, after in zip(packed, STEPS, ((near, sent0[5]), (far, sent0[6]), sent0[4]))
    ]
    table0, table1, stack0, stack1, back0, back1 = setup_call(slots, meta, white, near, far)

    own = lax.dynamic_index_in_dim(obs, me, 1, keepdims=False)
    own_sum, near_sum, far_sum = tile_call(table0, [own] + sent0, stack0, back0)
    sums0 = own_sum, send(near_sum, route_along(1)), send(far_sum, route_along(2))
    sent1, sums0 = lax.optimization_barrier((sent1, sums0))
    held = collect_call(1, place, whole_obs, pair, sent1)
    distant, far_sum = side_call(2 * blocks, reach, table1, held, stack1, back1)
    far_sum, held = lax.optimization_barrier((far_sum, held))
    far_sum = send(far_sum, route_along(2))
    close, near_sum = side_call(blocks, blocks, table1, held, stack1, back1)
    near_sum = send(near_sum, route_along(1))
    own_sum = nearby_call(table1, held, stack1, back1, close, distant)
    grad = final_call(mine, sums0, (own_sum, near_sum, far_sum))
    grad = lax.all_to_all(grad, "prow", split_axis=0, concat_axis=0, tiled=True)
    whole = grad.transpose(2, 3, 1, 0, 4).reshape(blocks, share, bins, parts, windows)
    return whole.astype(jnp.float32)


def solution(mesh):
    placed = (
        P("pcol", "prow", None, None, None),
        P("prow", "pcol", None, None),
        P("prow", "pcol"),
        P("prow", "pcol", None, None, None, None, None),
    )
    return jax.shard_map(
        local,
        mesh=mesh,
        in_specs=placed,
        out_specs=P("pcol", "prow", None, None, None),
        check_vma=False,
    )
```

```python
import functools

import jax
import jax.numpy as jnp
from jax import lax
from jax.experimental import pallas as pl
from jax.experimental.pallas import tpu as pltpu
from jax.sharding import PartitionSpec as P

BAND = 8
EPS = 1e-06
CURVE = 100.0
HOPS = ((1, 0), (3, 0), (1, 1), (3, 1), (0, 1), (2, 0), (2, 1))
STEPS = (1, 3, 2)
PLACES = (0, 2, 4, 3, 5, 1, 6, 7)
VMEM = pl.BlockSpec(memory_space=pltpu.VMEM)
SMEM = pl.BlockSpec(memory_space=pltpu.SMEM)
ANY = pl.BlockSpec(memory_space=pl.ANY)
HBM = pl.BlockSpec(memory_space=pltpu.HBM)
COPY_PARAMS = pltpu.CompilerParams(vmem_limit_bytes=46 * 1024 * 1024)
PARAMS = pltpu.CompilerParams(vmem_limit_bytes=40 * 1024 * 1024)


def setup_kernel(slots, meta, own, near, far, table0, table1, stack0, stack1, back0, back1):
    blocks, width, depth = own.shape[1:]
    reach = far.shape[1]
    span = blocks + reach + 1
    half = depth // 2
    for i in range(blocks * span):
        table0[i] = -1
        table1[i] = -1
    for k in range(8):

        def put(s, carry, k=k):
            a = meta[k, 1 + 2 * s]
            spot = a * span + meta[k, 2 + 2 * s] - a
            table0[spot] = k * slots + s
            table1[spot] = PLACES[k] * slots + s
            return carry

        lax.fori_loop(0, meta[k, 0], put, 0)
    for j, (stack, back) in enumerate(((stack0, back0), (stack1, back1))):
        for n in range(2 * blocks + reach):
            if n < blocks:
                block = own[j, n]
            elif n < 2 * blocks:
                block = near[j, n - blocks]
            else:
                block = far[j, n - 2 * blocks]
            turned = jnp.concatenate([block[:, half:], -block[:, :half]], axis=1)
            stack[n, :width] = block
            stack[n, width:] = turned
            if n < blocks:
                back[n, :width] = block
                back[n, width:] = -turned


def setup_call(slots, meta, own, near, far):
    blocks, width, depth = own.shape[1:]
    reach = far.shape[1]
    total = 2 * blocks + reach
    stack = jax.ShapeDtypeStruct((total, 2 * width, depth), own.dtype)
    back = jax.ShapeDtypeStruct((blocks, 2 * width, depth), own.dtype)
    return pl.pallas_call(
        functools.partial(setup_kernel, slots),
        out_shape=(
            jax.ShapeDtypeStruct((blocks * (blocks + reach + 1),), jnp.int32),
            jax.ShapeDtypeStruct((blocks * (blocks + reach + 1),), jnp.int32),
            stack,
            stack,
            back,
            back,
        ),
        in_specs=[SMEM, VMEM, VMEM, VMEM],
        out_specs=(SMEM, SMEM, VMEM, VMEM, VMEM, VMEM),
        compiler_params=PARAMS,
        name="setup",
    )(meta, own, near, far)


def slopes_of(table, held, upper, span, sums, b, low, high):
    width = upper.shape[0]
    pairs = []
    for a in range(low, high):
        spot = table[a * span + b - a]
        keep = spot >= 0
        spot = jnp.maximum(spot, 0)
        if a == high - 1:
            keep = jnp.logical_and(keep, jnp.logical_or(upper, a != b))
        halves = []
        for part in range(2):
            seen = held[spot, part].astype(jnp.float32) * width
            place = (a - low) * width
            diff = sums[place : place + width, part * width : (part + 1) * width] - seen
            slope = diff * lax.rsqrt(diff * diff * CURVE + float(width * width))
            halves.append(jnp.where(keep, slope, 0.0).astype(jnp.bfloat16))
        pairs.append(halves)
    return pairs


def products(back, block, low, high):
    width = back.shape[1] // 2
    rows = jnp.concatenate([back[a, :width] for a in range(low, high)], axis=0)
    return lax.dot_general(
        rows, block, (((1,), (1,)), ((), ())), preferred_element_type=jnp.float32
    )


def turned_product(slopes, back, a, first, last):
    left = jnp.concatenate([slopes[a, d] for d in range(first, last)], axis=1)
    return lax.dot_general(
        left, back[a], (((0,), (0,)), ((), ())), preferred_element_type=jnp.float32
    )


def upper_of(width):
    return lax.broadcasted_iota(jnp.int32, (width, width), 1) > lax.broadcasted_iota(
        jnp.int32, (width, width), 0
    )


def row_range(b, blocks, span):
    return max(0, b - span + 1), min(blocks, b + 1)


def side_kernel(start, table, held, stack, back, slopes, out, grad):
    blocks, double, depth = back.shape
    width = double // 2
    reach = stack.shape[0] - 2 * blocks
    span = blocks + reach + 1
    count = out.shape[0]
    upper = upper_of(width)
    grad[...] = jnp.zeros_like(grad)

    def column(b, low, high):
        sums = products(back, stack[b], low, high)
        pairs = slopes_of(table, held, upper, span, sums, b, low, high)
        for a in range(low, high):
            for part in range(2):
                slopes[a, b - start, part * width : (part + 1) * width] = pairs[a - low][part]

    def full(b, carry):
        column(b, 0, blocks)
        return carry

    stop = start + count
    lax.fori_loop(start, max(start, min(stop, span)), full, 0)
    for b in range(max(start, span), stop):
        column(b, *row_range(b, blocks, span))
    for a in range(blocks):
        last = min(stop, a + span)
        if last <= start:
            continue
        add = turned_product(slopes, back, a, 0, last - start)
        for b in range(start, last):
            grad[b - start] += add[(b - start) * width : (b - start + 1) * width]
    out[...] = grad[...].astype(jnp.bfloat16)


def nearby_kernel(table, held, stack, back, close, distant, grad, fresh):
    blocks, double, depth = back.shape
    width = double // 2
    total = stack.shape[0]
    reach = total - 2 * blocks
    span = blocks + reach + 1
    upper = upper_of(width)
    grad[...] = jnp.zeros_like(grad)

    def rows(b, low, high, wide):
        add = jnp.dot(jnp.concatenate(wide, axis=0), stack[b], preferred_element_type=jnp.float32)
        for a in range(low, high):
            grad[a] += add[(a - low) * width : (a - low + 1) * width]

    for b in range(blocks):
        sums = products(back, stack[b], 0, b + 1)
        pairs = slopes_of(table, held, upper, span, sums, b, 0, b + 1)
        for a in range(b + 1):
            for part in range(2):
                fresh[a, b - a, part * width : (part + 1) * width] = pairs[a][part]
        rows(b, 0, b + 1, [jnp.concatenate(pair, axis=1) for pair in pairs])

    def kept(slopes, a, n):
        return jnp.concatenate([slopes[a, n, :width], slopes[a, n, width:]], axis=1)

    def full(b, carry):
        rows(b, 0, blocks, [kept(close, a, b - blocks) for a in range(blocks)])
        return carry

    lax.fori_loop(blocks, span, full, 0)
    for b in range(span, total):
        low, high = row_range(b, blocks, span)
        slopes, first = (close, blocks) if b < 2 * blocks else (distant, 2 * blocks)
        rows(b, low, high, [kept(slopes, a, b - first) for a in range(low, high)])
    for a in range(blocks):
        add = turned_product(fresh, back, a, 0, blocks - a)
        for d in range(blocks - a):
            grad[a + d] += add[d * width : (d + 1) * width]


def cost(tiles, width, depth):
    return pl.CostEstimate(
        flops=tiles * 6 * width * depth * depth,
        bytes_accessed=tiles * 512 * 1024,
        transcendentals=0,
    )


def side_call(start, count, table, held, stack, back):
    blocks, double, depth = back.shape
    width = double // 2
    return pl.pallas_call(
        functools.partial(side_kernel, start),
        out_shape=(
            jax.ShapeDtypeStruct((blocks, count, double, width), jnp.bfloat16),
            jax.ShapeDtypeStruct((count, width, depth), jnp.bfloat16),
        ),
        in_specs=[SMEM] + [VMEM] * 3,
        out_specs=(VMEM, VMEM),
        scratch_shapes=[pltpu.VMEM((count, width, depth), jnp.float32)],
        compiler_params=PARAMS,
        cost_estimate=cost(0, width, depth),
        name="side",
    )(table, held, stack, back)


def nearby_call(table, held, stack, back, close, distant):
    blocks, double, depth = back.shape
    width = double // 2
    return pl.pallas_call(
        nearby_kernel,
        out_shape=jax.ShapeDtypeStruct((blocks, width, depth), jnp.float32),
        in_specs=[SMEM] + [VMEM] * 5,
        out_specs=VMEM,
        scratch_shapes=[pltpu.VMEM((blocks, blocks, double, width), jnp.bfloat16)],
        compiler_params=PARAMS,
        cost_estimate=cost(0, width, depth),
        name="nearby",
    )(table, held, stack, back, close, distant)


def gather(pieces, held, sems):
    slots = pieces[0].shape[0]
    copies = [
        pltpu.make_async_copy(piece, held.at[pl.ds(k * slots, slots)], sems.at[k])
        for k, piece in enumerate(pieces)
    ]
    for copy in copies:
        copy.start()
    return copies


def collect_kernel(j, place, obs, pair, first, second, third, held, sems):
    slots = pair.shape[0]
    parts = [obs.at[:, j, place[0], place[1]], pair.at[:, place[0]], first, second, third]
    starts = [0, 1, 2, 4, 6]
    copies = [
        pltpu.make_async_copy(
            part, held.at[pl.ds(start * slots, part.shape[0])], sems.at[k]
        )
        for k, (part, start) in enumerate(zip(parts, starts))
    ]
    for copy in copies:
        copy.start()
    for copy in copies:
        copy.wait()


def collect_call(j, place, obs, pair, arrived):
    slots = pair.shape[0]
    return pl.pallas_call(
        functools.partial(collect_kernel, j),
        out_shape=jax.ShapeDtypeStruct((8 * slots,) + pair.shape[2:], pair.dtype),
        in_specs=[SMEM, HBM] + [ANY] * 4,
        out_specs=VMEM,
        scratch_shapes=[pltpu.SemaphoreType.DMA((5,))],
        compiler_params=PARAMS,
        name="collect",
    )(place, obs, pair, *arrived)


def swap_kernel(j, place, obs, out, sem):
    copy = pltpu.make_async_copy(obs.at[:, j, :, 1 - place[1]], out, sem)
    copy.start()
    copy.wait()


def swap_call(j, place, obs):
    slots, _, chips = obs.shape[:3]
    return pl.pallas_call(
        functools.partial(swap_kernel, j),
        out_shape=jax.ShapeDtypeStruct((slots, chips) + obs.shape[4:], obs.dtype),
        in_specs=[SMEM, HBM],
        out_specs=VMEM,
        scratch_shapes=[pltpu.SemaphoreType.DMA(())],
        compiler_params=COPY_PARAMS,
        name="swap",
    )(place, obs)


def pack_kernel(j, place, obs, pair, first, second, third, sems):
    chips = pair.shape[1]
    copies = []
    for k, (step, out) in enumerate(zip(STEPS, (first, second, third))):
        chip = lax.rem(place[0] + step, chips)
        copies.append((obs.at[:, j, chip, place[1]], out.at[pl.ds(0, out.shape[0] // 2)], 2 * k))
        copies.append((pair.at[:, chip], out.at[pl.ds(out.shape[0] // 2, out.shape[0] // 2)], 2 * k + 1))
    copies = [pltpu.make_async_copy(src, dst, sems.at[k]) for src, dst, k in copies]
    for copy in copies:
        copy.start()
    for copy in copies:
        copy.wait()


def pack_call(j, place, obs, pair):
    slots = pair.shape[0]
    out = jax.ShapeDtypeStruct((2 * slots,) + pair.shape[2:], pair.dtype)
    return pl.pallas_call(
        functools.partial(pack_kernel, j),
        out_shape=(out, out, out),
        in_specs=[SMEM, HBM, ANY],
        out_specs=(VMEM, VMEM, VMEM),
        scratch_shapes=[pltpu.SemaphoreType.DMA((6,))],
        compiler_params=COPY_PARAMS,
        name="pack",
    )(place, obs, pair)


def tile_kernel(table, *refs):
    stack, back, grad_own, grad_near, grad_far, held, slopes, grad, sems = refs[8:]
    blocks, double, _ = back.shape
    width = double // 2
    total = stack.shape[0]
    reach = total - 2 * blocks
    span = blocks + reach + 1
    copies = gather(refs[:8], held, sems)
    grad[...] = jnp.zeros_like(grad)
    upper = upper_of(width)
    for copy in copies:
        copy.wait()

    def column(b, low, high):
        pairs = slopes_of(
            table, held, upper, span, products(back, stack[b], low, high), b, low, high
        )
        wide = []
        for a in range(low, high):
            for part in range(2):
                slopes[a, b - a, part * width : (part + 1) * width] = pairs[a - low][part]
            wide.append(jnp.concatenate(pairs[a - low], axis=1))
        add = jnp.dot(jnp.concatenate(wide, axis=0), stack[b], preferred_element_type=jnp.float32)
        for a in range(low, high):
            grad[a] += add[(a - low) * width : (a - low + 1) * width]

    for b in range(blocks - 1):
        column(b, 0, b + 1)

    def full(b, carry):
        column(b, 0, blocks)
        return carry

    lax.fori_loop(blocks - 1, span, full, 0)
    for b in range(span, total):
        column(b, *row_range(b, blocks, span))

    def mirror(a, carry):
        add = turned_product(slopes, back, a, 0, span)
        for d in range(span):
            grad[a + d] += add[d * width : (d + 1) * width]
        return carry

    lax.fori_loop(0, blocks, mirror, 0)
    grad_own[...] = grad[:blocks]
    grad_near[...] = grad[blocks : 2 * blocks].astype(jnp.bfloat16)
    grad_far[...] = grad[2 * blocks :].astype(jnp.bfloat16)


def tile_call(table, pieces, stack, back):
    slots = pieces[0].shape[0]
    blocks, double, depth = back.shape
    width = double // 2
    total = stack.shape[0]
    reach = total - 2 * blocks
    span = blocks + reach + 1
    return pl.pallas_call(
        tile_kernel,
        out_shape=(
            jax.ShapeDtypeStruct((blocks, width, depth), jnp.float32),
            jax.ShapeDtypeStruct((blocks, width, depth), jnp.bfloat16),
            jax.ShapeDtypeStruct((reach, width, depth), jnp.bfloat16),
        ),
        in_specs=[SMEM] + [ANY] * 8 + [VMEM] * 2,
        out_specs=(VMEM, VMEM, VMEM),
        scratch_shapes=[
            pltpu.VMEM((8 * slots, 2, width, width), jnp.bfloat16),
            pltpu.VMEM((blocks, span, double, width), jnp.bfloat16),
            pltpu.VMEM((total, width, depth), jnp.float32),
            pltpu.SemaphoreType.DMA((8,)),
        ],
        compiler_params=PARAMS,
        cost_estimate=cost(0, width, depth),
        name="tiles",
    )(table, *pieces, stack, back)


def final_kernel(spectra, own0, near0, far0, own1, near1, far1, out):
    for j, (own, near, far) in enumerate(((own0, near0, far0), (own1, near1, far1))):
        blocks = own.shape[0]
        reach = far.shape[0]
        scale = 2.0 / spectra.shape[-1]
        for n in range(blocks):
            values = spectra[j, n].astype(jnp.float32)
            power = jnp.sum(values * values, axis=1, keepdims=True) * scale
            factor = lax.rsqrt(power + EPS)
            total = own[n] + near[n].astype(jnp.float32)
            if n < reach:
                total = total + far[n].astype(jnp.float32)
            inner = jnp.sum(total * values, axis=1, keepdims=True) * scale
            grad = factor * total - values * (factor * factor * factor * inner)
            share = grad.shape[0] // 8
            for r in range(8):
                out[r, j, n] = grad[r * share : (r + 1) * share].astype(jnp.bfloat16)


def final_call(spectra, sums0, sums1):
    _, blocks, width, depth = spectra.shape
    return pl.pallas_call(
        final_kernel,
        out_shape=jax.ShapeDtypeStruct((8, 2, blocks, width // 8, depth), jnp.bfloat16),
        in_specs=[VMEM] * 7,
        out_specs=VMEM,
        compiler_params=PARAMS,
        name="final",
    )(spectra, *sums0, *sums1)


def route_across(step, flip):
    chips = lax.axis_size("prow") // 2
    return "prow", [
        (2 * y + c, 2 * ((y + step) % chips) + (c ^ flip)) for y in range(chips) for c in range(2)
    ]


def route_along(distance):
    devices = range(lax.axis_size("pcol"))
    return "pcol", [(i - distance, i) for i in devices if i - distance in devices]


def send(values, route, after=None):
    if after is not None:
        values, _ = lax.optimization_barrier((values, after))
    return lax.ppermute(values, *route)


def local(spectra, tile_list, tile_count, observed):
    blocks, share, bins, parts, windows = spectra.shape
    slots = tile_list.shape[2]
    width = 8 * share
    depth = parts * windows
    reach = BAND - blocks
    me = lax.axis_index("prow")
    chip = me // 2
    core = me % 2
    base = lax.axis_index("pcol") * blocks
    targets = [(chip + step) % 4 * 2 + (core ^ flip) for step, flip in HOPS]
    lists = [me] + [(chip - step) % 4 * 2 + (core ^ flip) for step, flip in HOPS]
    routes = [route_across(*hop) for hop in HOPS]
    obs = observed[0, 0]

    def cut(data, j, k):
        return lax.dynamic_index_in_dim(data, 8 * j + targets[k], 1, keepdims=False)

    early = [cut(obs, 0, k) for k in range(2)]
    early, spectra, obs = lax.optimization_barrier((early, spectra, obs))
    meta = jnp.concatenate([tile_count.reshape(1), (tile_list - base).reshape(-1)])
    count = meta.shape[0]
    meta = jnp.pad(meta.astype(jnp.bfloat16).reshape(1, count), ((0, share - 1), (0, depth - count)))
    load = spectra.reshape(blocks, share, 2, 8, depth).transpose(3, 2, 0, 1, 4)
    load = load.reshape(8, 2 * blocks, share, depth)
    load = jnp.concatenate([load, jnp.broadcast_to(meta, (8, 1) + meta.shape)], axis=1)

    load = lax.all_to_all(load, "prow", split_axis=0, concat_axis=0, tiled=True)
    parts0 = early + [cut(obs, 0, k) for k in range(2, 4)]
    _, obs = lax.optimization_barrier((parts0[2:], obs))
    parts0 += [cut(obs, 0, k) for k in range(4, 7)]
    load, _ = lax.optimization_barrier((load, parts0))
    sent0 = [send(parts0[k], routes[k]) for k in range(4)]
    sent0.append(send(parts0[4], routes[4], sent0[0]))
    sent0.append(send(parts0[5], routes[5], sent0[0]))
    sent0.append(send(parts0[6], routes[6], sent0[1]))
    whole_obs = observed.reshape((slots, 2, 4, 2) + observed.shape[4:])
    place = jnp.stack([chip, core])
    place, _ = lax.optimization_barrier((place, parts0[2:4]))
    swapped = swap_call(1, place, whole_obs)
    load, swapped = lax.optimization_barrier((load, swapped))
    pair = send(swapped, route_across(0, 1), sent0[:4])
    meta = load[:, -1, 0, :count].astype(jnp.int32)[jnp.stack(lists)]
    mine = load[:, :-1].reshape(8, 2, blocks, share, depth)
    mine = mine.transpose(1, 2, 0, 3, 4).reshape(2, blocks, width, depth)
    values = mine.astype(jnp.float32)
    power = jnp.sum(values * values, axis=-1, keepdims=True) / windows
    white = (values * lax.rsqrt(power + EPS)).astype(jnp.bfloat16)
    near = send(white, route_along(-1))
    far = send(white[:, :reach], route_along(-2))
    packed = pack_call(1, place, whole_obs, pair)
    sent1 = [
        send(part, route_across(step, 0), after)
        for part, step, after in zip(packed, STEPS, ((near, sent0[5]), (far, sent0[6]), sent0[4]))
    ]
    table0, table1, stack0, stack1, back0, back1 = setup_call(slots, meta, white, near, far)

    own = lax.dynamic_index_in_dim(obs, me, 1, keepdims=False)
    own_sum, near_sum, far_sum = tile_call(table0, [own] + sent0, stack0, back0)
    sums0 = own_sum, send(near_sum, route_along(1)), send(far_sum, route_along(2))
    sent1, sums0 = lax.optimization_barrier((sent1, sums0))
    held = collect_call(1, place, whole_obs, pair, sent1)
    distant, far_sum = side_call(2 * blocks, reach, table1, held, stack1, back1)
    far_sum, held = lax.optimization_barrier((far_sum, held))
    far_sum = send(far_sum, route_along(2))
    close, near_sum = side_call(blocks, blocks, table1, held, stack1, back1)
    near_sum = send(near_sum, route_along(1))
    own_sum = nearby_call(table1, held, stack1, back1, close, distant)
    grad = final_call(mine, sums0, (own_sum, near_sum, far_sum))
    grad = lax.all_to_all(grad, "prow", split_axis=0, concat_axis=0, tiled=True)
    whole = grad.transpose(2, 3, 1, 0, 4).reshape(blocks, share, bins, parts, windows)
    return whole.astype(jnp.float32)


def solution(mesh):
    placed = (
        P("pcol", "prow", None, None, None),
        P("prow", "pcol", None, None),
        P("prow", "pcol"),
        P("prow", "pcol", None, None, None, None, None),
    )
    return jax.shard_map(
        local,
        mesh=mesh,
        in_specs=placed,
        out_specs=P("pcol", "prow", None, None, None),
        check_vma=False,
    )
```
